128 devices in a mesh: ka: 4 (over x_hi, core), vert: 32 (over y, x_lo, z).
Axes of the slice: x: 4 (x_hi: 2, x_lo: 2; x = x_hi * 2 + x_lo), y: 4, z: 4, core: 2. Of those that a mesh axis runs over, the one named last changes fastest.
Arguments:
- eig_lower: bfloat16 [512, 65536], P(None, ('ka', 'vert')), may hold values from -6 to 6
- eig_upper: bfloat16 [256, 65536], P(None, ('ka', 'vert')), may hold values from -6 to 6
- layout_map: int32 [65536], replicated, may hold values from 0 to 65535, as said below
- block_live: int32 [8], replicated, may hold values from 1 to 8192, 40960 in all
- coupling: int32 [8, 3], replicated, may hold values 0 or 1
- rot_coef: float32 [8, 3], replicated, may hold values from -4 to 4
- dip_zero: bfloat16 [8192, 8192], P('vert', 'ka'), may hold values from -0.00030517578 to 0.00030517578
- dip_raise: bfloat16 [8192, 8192], P('vert', 'ka'), may hold values from -0.00030517578 to 0.00030517578
- dip_lower: bfloat16 [8192, 8192], P('vert', 'ka'), may hold values from -0.00030517578 to 0.00030517578
Outputs:
- strength: float32 [512, 256], P('ka', 'vert')
The draws below stay inside these ranges and needn't reach their ends.
Inputs may be any that keep to these rules, and one draw needn't show every extreme that they name: layout_map is a permutation of 0 to 65535 made of runs of 128 solver rows that hold 128 consecutive basis rows beginning at a multiple of 128. The solver rows lie on the devices of ka+vert in runs of 512, in device order; each run holds exactly 128 basis rows of each range of 16384 consecutive basis rows. `block_live`: the sizes sum to 40960; one of them is 8192.
All inputs are finite; a program needn't handle non-finite values.
Results may differ from the reference program's by a relative error of at most 0.0033.
Values may be sent and summed in bfloat16 or wider, within the bound.
A program may use at most 128 MiB of HBM per device.

```python
import math
import jax
import jax.numpy as jnp
import numpy as np

NV = 8192
NK = 8
NI = 512
NF = 256
R = 65536
BLOCK = 128
N_KA = 4
DEVICES = 128


def draw_layout_map(key, part):
    key = jax.random.fold_in(key, 11)
    owner_rows = NK * NV // N_KA
    owner_slot = owner_rows // DEVICES
    run_rows = BLOCK
    owner_runs = owner_rows // run_rows
    slot_runs = owner_slot // run_rows
    subkeys = jax.random.split(key, N_KA + DEVICES)

    def owner_order(subkey):
        return jax.random.permutation(subkey, owner_runs)

    def device_order(subkey):
        return jax.random.permutation(subkey, N_KA * slot_runs)
    per_owner = jax.vmap(owner_order)(subkeys[:N_KA])
    per_owner = per_owner + (jnp.arange(N_KA) * owner_runs)[:, None]
    dealt = per_owner.reshape(N_KA, DEVICES, slot_runs).transpose(1, 0, 2).reshape(DEVICES, N_KA * slot_runs)
    shuffles = jax.vmap(device_order)(subkeys[N_KA:])
    mixed = jnp.take_along_axis(dealt, shuffles, axis=1)
    rows = mixed[:, :, None] * run_rows + jnp.arange(run_rows)[None, None, :]
    return rows.reshape(-1).astype(jnp.int32)


def with_ends(array, own_key, least, top_value):
    longest = array.shape.index(max(array.shape))
    spots = []
    for shift in (0, 1):
        where = [jax.random.randint(jax.random.fold_in(own_key, axis), (), 0, length) for axis, length in enumerate(array.shape)]
        where[longest] = (where[longest] + shift) % array.shape[longest]
        spots.append(tuple(where))
    return array.at[spots[0]].set(least).at[spots[1]].set(top_value)


def steps_of(stream_key, dims, cuts, smallest, largest):
    level, own = 1.0, jax.random.fold_in(stream_key, 6)
    for dim, shards_of in cuts:
        draws = jnp.exp(jax.random.uniform(jax.random.fold_in(own, dim), (shards_of,), jnp.float32, smallest / len(cuts), largest / len(cuts)))
        level = level * jnp.repeat(draws, dims[dim] // shards_of).reshape([-1 if axis == dim else 1 for axis in range(len(dims))])
    return level


def length_profile(amount, total, limit, skew):
    weights = [(1 << 20) // math.isqrt(rank ** skew) + 1 for rank in range(2, amount + 1)]
    spare, given = total - limit - (amount - 1), [1] * (amount - 1)
    while spare > 0:
        free = [i for i in range(amount - 1) if given[i] < limit]
        mass, budget = sum([weights[i] for i in free]), spare
        for i in free:
            more = min(limit - given[i], max(1, budget * weights[i] // mass), spare)
            given[i] = given[i] + more
            spare = spare - more
    return np.array([limit] + given)


def uneven_parts(key, amount, total, bound, slope):
    if amount == 2:
        one = jax.random.randint(key, (), max(1, total - bound), min(bound, total - 1) + 1)
        return jnp.stack([one, total - one])
    lengths = jnp.asarray(length_profile(amount, total, bound, slope), jnp.int32)
    couples = (amount - 1) // 2
    giver, taker = lengths[1:1 + 2 * couples:2], lengths[2:2 + 2 * couples:2]
    room = jnp.minimum(giver - 1, bound - taker)
    passed = jax.random.randint(jax.random.fold_in(key, 1), (couples,), 0, 1 << 20) % (room + 1)
    lengths = lengths.at[1:1 + 2 * couples:2].set(giver - passed).at[2:2 + 2 * couples:2].set(taker + passed)
    return lengths[jax.random.permutation(jax.random.fold_in(key, 2), amount)]


def scatter_about(rng, shape, deviation, limit, pieces=(), kind=jnp.bfloat16):
    gain = steps_of(rng, shape, pieces, -0.22, 0.18) if pieces else 1.0
    entries = jax.random.normal(rng, shape, jnp.float32) * deviation * gain
    return jnp.minimum(jnp.maximum(entries, -limit), limit).astype(kind)


def setup_inputs(seed: int = 0) -> dict:
    seeds = jax.random.split(jax.random.key(seed), 10)
    return {
        "eig_lower": scatter_about(seeds[0], (NI, R), 1.0, 6.0, ((1, 128),)),
        "eig_upper": scatter_about(seeds[1], (NF, R), 1.0, 6.0, ((1, 128),)),
        "layout_map": draw_layout_map(jax.random.fold_in(seeds[9], 71), 0),
        "block_live": uneven_parts(seeds[3], NK, 5 * NV, NV, 0).astype(jnp.int32),
        "coupling": with_ends((jax.random.randint(seeds[4], (NK, 3), 0, 4) < 3).astype(jnp.int32), jax.random.fold_in(seeds[4], 1), 0, 1),
        "rot_coef": scatter_about(seeds[5], (NK, 3), 1.0, 4.0, (), jnp.float32),
        "dip_zero": scatter_about(seeds[6], (NV, NV), (6 * NV * NV) ** -0.5, 0.00030517578, ((0, 32), (1, 4))),
        "dip_raise": scatter_about(seeds[7], (NV, NV), (6 * NV * NV) ** -0.5, 0.00030517578, ((0, 32), (1, 4))),
        "dip_lower": scatter_about(seeds[8], (NV, NV), (6 * NV * NV) ** -0.5, 0.00030517578, ((0, 32), (1, 4))),
    }


def combine_terms(upper_range, mat_zero, mat_raise, mat_lower, factors):
    upper_f = upper_range.astype(jnp.float32)
    term_zero = jnp.einsum('fkc,rc->fkr', upper_f, mat_zero.astype(jnp.float32))
    term_raise = jnp.einsum('fkc,rc->fkr', upper_f, mat_raise.astype(jnp.float32))
    term_lower = jnp.einsum('fkc,rc->fkr', upper_f, mat_lower.astype(jnp.float32))
    edge_zero = jnp.zeros_like(term_zero[:, :1])
    raised = jnp.concatenate([term_raise[:, 1:], edge_zero], axis=1)
    lowered = jnp.concatenate([edge_zero, term_lower[:, :-1]], axis=1)
    return (factors[:, 0][None, :, None] * term_zero
            + factors[:, 1][None, :, None] * raised
            + factors[:, 2][None, :, None] * lowered)


def reference(eig_lower, eig_upper, layout_map, block_live, coupling, rot_coef, dip_zero, dip_raise, dip_lower):
    inverse = jnp.argsort(layout_map).astype(jnp.int32)
    vib_index = jnp.arange(NV, dtype=jnp.int32)
    live_mask = vib_index[None, :] < block_live[:, None]

    def arrange(vectors):
        in_basis = jnp.take(vectors, inverse, axis=1).reshape(vectors.shape[0], NK, NV)
        return jnp.where(live_mask[None], in_basis, jnp.zeros_like(in_basis))

    lower_vec = arrange(eig_lower)
    upper_vec = arrange(eig_upper)
    factors = rot_coef * coupling.astype(jnp.float32)
    range_width = NV // N_KA
    lower_wide = lower_vec.astype(jnp.float32)
    amplitude = jnp.zeros((eig_lower.shape[0], eig_upper.shape[0]), jnp.float32)
    for range_index in range(N_KA):
        low_edge = range_index * range_width
        upper_range = upper_vec[:, :, low_edge:low_edge + range_width]
        half_block = combine_terms(upper_range,
                                   dip_zero[:, low_edge:low_edge + range_width],
                                   dip_raise[:, low_edge:low_edge + range_width],
                                   dip_lower[:, low_edge:low_edge + range_width],
                                   factors).astype(jnp.bfloat16)
        amplitude = amplitude + jnp.einsum('ikr,fkr->if', lower_wide, half_block.astype(jnp.float32))
    return amplitude * amplitude
```

```python
import jax
import jax.numpy as jnp
from jax import lax
from jax.experimental import pallas as pl
from jax.experimental.pallas import tpu as pltpu
from jax.sharding import PartitionSpec as P

F32 = jnp.float32
BF16 = jnp.bfloat16
MESH = pl.DeviceIdType.MESH
WIDTHS = (768, 768, 256, 256)
STARTS = (0, 768, 1536, 1792)
ORDERS = ("xyz", "xzy", "yzx", "zyx")
NT = (((1,), (1,)), ((), ()))


def kernel(
    head_ref, src_ref, live_ref, coup_ref, rot_ref, low_ref, up_ref, dz_hbm, dr_hbm, dl_hbm,
    out_ref,
    send_buf, recv_buf, sta, stb, stc, std_, ua, ub, uc, ud, stage_low, low_all, dip, half, amp, parts,
    dip_sem, a_send, a_recv, q_send, q_recv, g_send, g_recv, l_send, l_recv, m_send, m_recv, r_send, r_recv,
):
    ka = lax.axis_index("ka")
    vert = lax.axis_index("vert")
    me = ka * 32 + vert
    yy = vert // 8
    xx = (vert // 4) % 2
    zz = vert % 4
    stages = (sta, stb, stc, std_)
    uppers = (ua, ub, uc, ud)

    barrier = pltpu.get_barrier_semaphore()

    def greet(k, _):
        pl.semaphore_signal(
            barrier, inc=1, device_id=((ka + k // 32) % 4, (vert + k % 32) % 32), device_id_type=MESH
        )
        return 0

    lax.fori_loop(1, 128, greet, 0)
    dips = [pltpu.make_async_copy(h, dip.at[n], dip_sem.at[n]) for n, h in enumerate((dz_hbm, dr_hbm, dl_hbm))]
    for c in dips:
        c.start()

    lane = lax.broadcasted_iota(jnp.int32, (8, 128), 1)
    zeros = jnp.zeros((8, 128), jnp.int32)
    heads = [zeros + head_ref[me * 4 + r] for r in range(4)]
    owned = [[(heads[r] >= o * 128) & (heads[r] < (o + 1) * 128) for r in range(3)] for o in range(4)]

    def pack(j, _):
        for u in range(3):
            unit = up_ref[j] if u == 0 else low_ref[2 * j + u - 1]
            runs = [unit[:, r * 128:(r + 1) * 128].astype(F32) for r in range(4)]
            for o in range(4):
                value = runs[3]
                for r in range(3):
                    value = jnp.where(owned[o][r], runs[r], value)
                send_buf[o * 32 + j, u] = value.astype(BF16)
        return 0

    lax.fori_loop(0, 32, pack, 0)
    pl.semaphore_wait(barrier, 127)

    def spread(k, _):
        ka2, v2 = (ka + k // 32) % 4, (vert + k % 32) % 32
        pltpu.make_async_remote_copy(
            src_ref=send_buf.at[ka2 * 32 + v2], dst_ref=recv_buf.at[me],
            send_sem=a_send, recv_sem=a_recv, device_id=(ka2, v2), device_id_type=MESH,
        ).start()
        return 0

    lax.fori_loop(1, 128, spread, 0)
    recv_buf[me] = send_buf[me]
    pltpu.make_async_copy(recv_buf.at[pl.ds(0, 127)], recv_buf.at[pl.ds(0, 127)], a_recv).wait()

    lives = [live_ref[2 * ka + b] for b in range(2)]

    def arrange_up(q, _):
        for n in range(16):
            block = q * 16 + n
            halves = []
            for b in range(2):
                s = src_ref[ka * 128 + b * 64 + block]
                tile = recv_buf[s, 0].astype(F32)
                halves.append(jnp.where(lane + block * 128 < lives[b], tile, 0.0))
            both = jnp.concatenate(halves, axis=0).astype(BF16)
            for c in range(4):
                if STARTS[c] <= n * 128 < STARTS[c] + WIDTHS[c]:
                    at = n * 128 - STARTS[c]
                    stages[c][q, :, at:at + 128] = both
        return 0

    lax.fori_loop(0, 4, arrange_up, 0)

    exchanges = []
    for c in range(4):
        row = []
        for d in range(1, 4):
            q = (ka + d) % 4
            copy = pltpu.make_async_remote_copy(
                src_ref=stages[c].at[q], dst_ref=uppers[c].at[yy, xx, zz, ka],
                send_sem=q_send.at[c, d - 1], recv_sem=q_recv.at[c, d - 1],
                device_id=(q, vert), device_id_type=MESH,
            )
            copy.start()
            row.append(copy)
        exchanges.append(row)
        uppers[c][yy, xx, zz, ka] = stages[c][ka]

    def arrange_low(v, _):
        for b in range(2):
            for h in range(2):
                block = 2 * v + h
                s = src_ref[ka * 128 + b * 64 + block]
                keep = lane + block * 128 < lives[b]
                both = jnp.concatenate(
                    [jnp.where(keep, recv_buf[s, u].astype(F32), 0.0) for u in (1, 2)], axis=0
                ).astype(BF16)
                at = b * 256 + h * 128
                stage_low[v, :, at:at + 128] = both
        return 0

    lax.fori_loop(0, 32, arrange_low, 0)

    def spread_low(k, _):
        v2 = (vert + k) % 32
        pltpu.make_async_remote_copy(
            src_ref=stage_low.at[v2], dst_ref=low_all.at[ka, vert],
            send_sem=l_send, recv_sem=l_recv, device_id=(ka, v2), device_id_type=MESH,
        ).start()
        return 0

    lax.fori_loop(1, 32, spread_low, 0)
    low_all[ka, vert] = stage_low[vert]

    def vid(y, x, z):
        return y * 8 + x * 4 + z

    sent = []

    def chain(c):
        u = uppers[c]
        where = {"y": yy, "x": xx, "z": zz}
        have = {"y": False, "x": False, "z": False}
        count = 0

        def region(fixed):
            idx = []
            for name, size in (("y", 4), ("x", 2), ("z", 4)):
                if name in fixed:
                    idx.append(fixed[name])
                elif have[name]:
                    idx.append(pl.ds(0, size))
                else:
                    idx.append(where[name])
            return u.at[tuple(idx)]

        def go(ref, axis, step):
            nonlocal count
            size = 2 if axis == "x" else 4
            to = dict(where)
            to[axis] = (where[axis] + step) % size
            copy = pltpu.make_async_remote_copy(
                src_ref=ref, dst_ref=ref, send_sem=g_send.at[c, count], recv_sem=g_recv.at[c, count],
                device_id=(ka, vid(to["y"], to["x"], to["z"])), device_id_type=MESH,
            )
            count += 1
            copy.start()
            sent.append(copy)
            return copy

        for axis in ORDERS[c]:
            here = where[axis]
            if axis == "x":
                one = go(region({"x": here}), "x", 1)
                yield
                one.wait_recv()
            else:
                plus = go(region({axis: here}), axis, 1)
                minus = go(region({axis: here}), axis, 3)
                yield
                before, after = (here + 3) % 4, (here + 1) % 4
                other = "z" if axis == "y" else "y"
                if have[other]:
                    first, second = {other: pl.ds(0, 2)}, {other: pl.ds(2, 2)}
                    cut = None
                elif have["x"]:
                    first, second = {"x": 0}, {"x": 1}
                    cut = None
                else:
                    first, second = {}, {}
                    cut = True
                plus.wait_recv()
                r1 = region({axis: before, **first})
                on1 = go(r1.at[pl.ds(0, 2)] if cut else r1, axis, 1)
                minus.wait_recv()
                r2 = region({axis: after, **second})
                on2 = go(r2.at[pl.ds(2, 2)] if cut else r2, axis, 3)
                yield
                on1.wait_recv()
                on2.wait_recv()
            have[axis] = True

    chains = [chain(c) for c in range(4)]

    def low_copy(slot, owner, to):
        return pltpu.make_async_remote_copy(
            src_ref=low_all.at[owner], dst_ref=low_all.at[owner],
            send_sem=m_send.at[slot], recv_sem=m_recv.at[slot], device_id=(to, vert), device_id_type=MESH,
        )

    sibling = (ka // 2) * 2 + (ka + 1) % 2
    across = (ka + 2) % 4
    moves = []
    for c in range(4):
        for copy in exchanges[c]:
            copy.wait_recv()
        next(chains[c])
    for c in (2, 3, 0, 1):
        next(chains[c])
    pltpu.make_async_copy(low_all.at[0, pl.ds(0, 31)], low_all.at[0, pl.ds(0, 31)], l_recv).wait()
    moves.append(low_copy(0, ka, sibling))
    moves.append(low_copy(1, ka, across))
    for m in moves:
        m.start()
    for c in (2, 3, 0, 1):
        next(chains[c])
    for c in (2, 3, 0, 1):
        next(chains[c])
    moves[1].wait_recv()
    moves.append(low_copy(2, across, sibling))
    moves[2].start()
    live_chains = [2, 3, 0, 1]
    while live_chains:
        for c in list(live_chains):
            if next(chains[c], "end") == "end":
                live_chains.remove(c)
    moves[0].wait_recv()
    moves[2].wait_recv()
    for c in dips:
        c.wait()

    def factor(k, d):
        return rot_ref[k, d] * coup_ref[k, d].astype(F32)

    def step(g, _):
        y, x = g // 2, g % 2
        sums = []
        for n in range(3):
            total = None
            for c in range(4):
                rows = uppers[c][y, x].reshape(256, WIDTHS[c])
                term = lax.dot_general(
                    rows, dip[n, :, STARTS[c]:STARTS[c] + WIDTHS[c]], NT, preferred_element_type=F32
                )
                total = term if total is None else total + term
            sums.append(total.reshape(4, 8, 8, 256))
        zero, up, down = sums
        rows = pl.ds(pl.multiple_of(g * 32, 32), 32)
        for k in range(8):
            value = factor(k, 0) * zero[:, k]
            if k < 7:
                value = value + factor(k, 1) * up[:, k + 1]
            if k > 0:
                value = value + factor(k, 2) * down[:, k - 1]
            half[rows, k * 256:(k + 1) * 256] = value.reshape(32, 256).astype(BF16)
        return 0

    lax.fori_loop(0, 8, step, 0)

    for t in range(4):
        total = None
        for o in range(4):
            lows = low_all[o, pl.ds(t * 8, 8)].reshape(128, 512)
            term = lax.dot_general(half[:, o * 512:(o + 1) * 512], lows, NT, preferred_element_type=F32)
            total = term if total is None else total + term
        amp[t] = total.reshape(32, 8, 128)

    def give(k, _):
        ka2, v2 = (ka + k // 32) % 4, (vert + k % 32) % 32
        pltpu.make_async_remote_copy(
            src_ref=amp.at[ka2, v2], dst_ref=parts.at[me],
            send_sem=r_send, recv_sem=r_recv, device_id=(ka2, v2), device_id_type=MESH,
        ).start()
        return 0

    lax.fori_loop(1, 128, give, 0)
    parts[me] = amp[ka, vert]
    pltpu.make_async_copy(parts.at[pl.ds(0, 127)], parts.at[pl.ds(0, 127)], r_recv).wait()
    total = jnp.sum(parts[...], axis=0)
    out_ref[...] = total * total

    pltpu.make_async_copy(send_buf.at[pl.ds(0, 127)], send_buf.at[pl.ds(0, 127)], a_send).wait()
    for row in exchanges:
        for copy in row:
            copy.wait_send()
    pltpu.make_async_copy(stage_low.at[pl.ds(0, 31)], stage_low.at[pl.ds(0, 31)], l_send).wait()
    for copy in sent + moves:
        copy.wait_send()
    pltpu.make_async_copy(parts.at[pl.ds(0, 127)], parts.at[pl.ds(0, 127)], r_send).wait()


def per_device(
    eig_lower, eig_upper, layout_map, block_live, coupling, rot_coef, dip_zero, dip_raise, dip_lower
):
    heads = layout_map.reshape(512, 128)[:, 0] // 128
    hits = heads[None, :] == jnp.arange(512, dtype=jnp.int32)[:, None]
    source = jnp.sum(jnp.where(hits, (jnp.arange(512, dtype=jnp.int32) // 4)[None, :], 0), axis=1)
    smem = pl.BlockSpec(memory_space=pltpu.SMEM)
    vmem = pl.BlockSpec(memory_space=pltpu.VMEM)
    hbm = pl.BlockSpec(memory_space=pl.ANY)
    dma = pltpu.SemaphoreType.DMA
    out = pl.pallas_call(
        kernel,
        out_shape=jax.ShapeDtypeStruct((8, 128), F32),
        in_specs=[smem] * 5 + [vmem] * 2 + [hbm] * 3,
        out_specs=vmem,
        scratch_shapes=[
            pltpu.VMEM((128, 3, 8, 128), BF16),
            pltpu.VMEM((128, 3, 8, 128), BF16),
            *[pltpu.VMEM((4, 16, w), BF16) for w in WIDTHS],
            *[pltpu.VMEM((4, 2, 4, 4, 16, w), BF16) for w in WIDTHS],
            pltpu.VMEM((32, 16, 512), BF16),
            pltpu.VMEM((4, 32, 16, 512), BF16),
            pltpu.VMEM((3, 256, 2048), BF16),
            pltpu.VMEM((256, 2048), BF16),
            pltpu.VMEM((4, 32, 8, 128), F32),
            pltpu.VMEM((128, 8, 128), F32),
            dma((3,)),
            dma, dma,
            dma((4, 3)), dma((4, 3)),
            dma((4, 9)), dma((4, 9)),
            dma, dma,
            dma((3,)), dma((3,)),
            dma, dma,
        ],
        compiler_params=pltpu.CompilerParams(
            collective_id=0, has_side_effects=True, vmem_limit_bytes=48 * 1024 * 1024
        ),
        cost_estimate=pl.CostEstimate(flops=7_000_000_000, bytes_accessed=5_000_000, transcendentals=0),
    )(
        heads, source, block_live, coupling, rot_coef,
        eig_lower.reshape(64, 8, 512), eig_upper.reshape(32, 8, 512), dip_zero, dip_raise, dip_lower,
    )
    return out.T


def solution(mesh):
    return jax.shard_map(
        per_device,
        mesh=mesh,
        in_specs=(
            P(None, ("ka", "vert")),
            P(None, ("ka", "vert")),
            P(),
            P(),
            P(),
            P(),
            P("vert", "ka"),
            P("vert", "ka"),
            P("vert", "ka"),
        ),
        out_specs=P("ka", "vert"),
        check_vma=False,
    )
```

```python
import jax
import jax.numpy as jnp
from jax import lax
from jax.experimental import pallas as pl
from jax.experimental.pallas import tpu as pltpu
from jax.sharding import PartitionSpec as P

F32 = jnp.float32
BF16 = jnp.bfloat16
MESH = pl.DeviceIdType.MESH
WIDTHS = (768, 768, 256, 256)
STARTS = (0, 768, 1536, 1792)
ORDERS = ("xyz", "xzy", "yzx", "zyx")
NT = (((1,), (1,)), ((), ()))


def kernel(
    head_ref, src_ref, live_ref, coup_ref, rot_ref, low_hbm, up_hbm, dz_hbm, dr_hbm, dl_hbm,
    out_ref,
    low_ref, up_ref, up_send, up_mid, up_recv, low_send, low_mid, low_recv,
    sta, stb, stc, std_, ua, ub, uc, ud, stage_low, low_all, dip, half, amp, part1, row_sum, part2,
    ready, in_sem, dip_sem, s1, r1, s2, r2, q_send, q_recv, g_send, g_recv, l_send, l_recv, m_send, m_recv,
):
    ka = lax.axis_index("ka")
    vert = lax.axis_index("vert")
    yy = vert // 8
    xx = (vert // 4) % 2
    zz = vert % 4
    row = ka * 2 + xx
    plane = yy * 4 + zz
    stages = (sta, stb, stc, std_)
    uppers = (ua, ub, uc, ud)

    def in_row(p):
        return p // 2, yy * 8 + (p % 2) * 4 + zz

    def in_plane(w):
        return ka, (w // 4) * 8 + xx * 4 + w % 4

    def say(sem, to):
        pl.semaphore_signal(sem, inc=1, device_id=to, device_id_type=MESH)

    def take(ref, sem):
        pltpu.make_async_copy(ref, ref, sem).wait()

    def send(src, dst, out_sem, in_sem_, to):
        copy = pltpu.make_async_remote_copy(
            src_ref=src, dst_ref=dst, send_sem=out_sem, recv_sem=in_sem_, device_id=to, device_id_type=MESH
        )
        copy.start()
        return copy

    barrier = pltpu.get_barrier_semaphore()
    for k in range(1, 8):
        say(barrier, in_row((row + k) % 8))
    for k in range(1, 4):
        say(barrier, in_plane(((yy + k) % 4) * 4 + zz))
        say(barrier, in_plane(yy * 4 + (zz + k) % 4))
    loads = [pltpu.make_async_copy(h, v, in_sem.at[n]) for n, (h, v) in enumerate(((up_hbm, up_ref), (low_hbm, low_ref)))]
    dips = [pltpu.make_async_copy(h, dip.at[n], dip_sem.at[n]) for n, h in enumerate((dz_hbm, dr_hbm, dl_hbm))]
    for c in loads + dips:
        c.start()
    for c in loads:
        c.wait()

    lane = lax.broadcasted_iota(jnp.int32, (8, 128), 1)
    zeros = jnp.zeros((8, 128), jnp.int32)
    heads = [zeros + head_ref[(ka * 32 + vert) * 4 + r] for r in range(4)]
    owned = [[(heads[r] >= o * 128) & (heads[r] < (o + 1) * 128) for r in range(3)] for o in range(4)]

    def pack(j, _):
        x2, w2 = (j // 4) % 2, (j // 8) * 4 + j % 4
        for u in range(3):
            unit = up_ref[j] if u == 0 else low_ref[2 * j + u - 1]
            runs = [unit[:, r * 128:(r + 1) * 128].astype(F32) for r in range(4)]
            for o in range(4):
                value = runs[3]
                for r in range(3):
                    value = jnp.where(owned[o][r], runs[r], value)
                if u == 0:
                    up_send[o * 2 + x2, w2] = value.astype(BF16)
                else:
                    low_send[w2, o * 2 + x2, u - 1] = value.astype(BF16)
        return 0

    lax.fori_loop(0, 32, pack, 0)
    pl.semaphore_wait(barrier, 13)

    for k in range(1, 8):
        p = (row + k) % 8
        send(up_send.at[p], up_mid.at[row], s1.at[0], r1.at[0], in_row(p))
    for k in range(1, 4):
        say(ready, in_plane(yy * 4 + (zz + k) % 4))
    up_mid[row] = up_send[row]
    pl.semaphore_wait(ready, 3)
    take(up_mid.at[pl.ds(0, 7)], r1.at[0])
    for k in range(1, 16):
        w = (plane + k) % 16
        send(up_mid.at[:, w], up_recv.at[plane], s2.at[0], r2.at[0], in_plane(w))
    up_recv[plane] = up_mid[:, plane]
    for k in range(1, 16):
        w = (plane + k) % 16
        send(low_send.at[w], low_mid.at[plane], s1.at[1], r1.at[1], in_plane(w))
    low_mid[plane] = low_send[plane]
    take(up_recv.at[pl.ds(0, 15)], r2.at[0])

    lives = [live_ref[2 * ka + b] for b in range(2)]

    def arrange_up(q, _):
        for n in range(16):
            block = q * 16 + n
            halves = []
            for b in range(2):
                s = src_ref[ka * 128 + b * 64 + block]
                tile = up_recv[s // 8, s % 8].astype(F32)
                halves.append(jnp.where(lane + block * 128 < lives[b], tile, 0.0))
            both = jnp.concatenate(halves, axis=0).astype(BF16)
            for c in range(4):
                if STARTS[c] <= n * 128 < STARTS[c] + WIDTHS[c]:
                    at = n * 128 - STARTS[c]
                    stages[c][q, :, at:at + 128] = both
        return 0

    lax.fori_loop(0, 4, arrange_up, 0)

    exchanges = []
    for c in range(4):
        copies = []
        for d in range(1, 4):
            q = (ka + d) % 4
            copies.append(send(
                stages[c].at[q], uppers[c].at[yy, xx, zz, ka], q_send.at[c, d - 1], q_recv.at[c, d - 1], (q, vert)
            ))
        exchanges.append(copies)
        uppers[c][yy, xx, zz, ka] = stages[c][ka]

    take(low_mid.at[pl.ds(0, 15)], r1.at[1])
    for k in range(1, 8):
        p = (row + k) % 8
        send(low_mid.at[:, p], low_recv.at[:, row], s2.at[1], r2.at[1], in_row(p))
    low_recv[:, row] = low_mid[:, row]

    def arrange_low(v, _):
        for b in range(2):
            for h in range(2):
                block = 2 * v + h
                s = src_ref[ka * 128 + b * 64 + block]
                keep = lane + block * 128 < lives[b]
                both = jnp.concatenate(
                    [jnp.where(keep, low_recv[s // 8, s % 8, u].astype(F32), 0.0) for u in range(2)], axis=0
                ).astype(BF16)
                at = b * 256 + h * 128
                stage_low[v, :, at:at + 128] = both
        return 0

    def spread_low(k, _):
        v2 = (vert + k) % 32
        send(stage_low.at[v2], low_all.at[ka, vert], l_send, l_recv, (ka, v2))
        return 0

    def vid(y, x, z):
        return y * 8 + x * 4 + z

    sent = []

    def chain(c):
        u = uppers[c]
        where = {"y": yy, "x": xx, "z": zz}
        have = {"y": False, "x": False, "z": False}
        count = 0

        def region(fixed):
            idx = []
            for name, size in (("y", 4), ("x", 2), ("z", 4)):
                if name in fixed:
                    idx.append(fixed[name])
                elif have[name]:
                    idx.append(pl.ds(0, size))
                else:
                    idx.append(where[name])
            return u.at[tuple(idx)]

        def go(ref, axis, step):
            nonlocal count
            size = 2 if axis == "x" else 4
            to = dict(where)
            to[axis] = (where[axis] + step) % size
            copy = pltpu.make_async_remote_copy(
                src_ref=ref, dst_ref=ref, send_sem=g_send.at[c, count], recv_sem=g_recv.at[c, count],
                device_id=(ka, vid(to["y"], to["x"], to["z"])), device_id_type=MESH,
            )
            count += 1
            copy.start()
            sent.append(copy)
            return copy

        for axis in ORDERS[c]:
            here = where[axis]
            if axis == "x":
                one = go(region({"x": here}), "x", 1)
                yield
                one.wait_recv()
            else:
                plus = go(region({axis: here}), axis, 1)
                minus = go(region({axis: here}), axis, 3)
                yield
                before, after = (here + 3) % 4, (here + 1) % 4
                other = "z" if axis == "y" else "y"
                if have[other]:
                    first, second = {other: pl.ds(0, 2)}, {other: pl.ds(2, 2)}
                    cut = None
                elif have["x"]:
                    first, second = {"x": 0}, {"x": 1}
                    cut = None
                else:
                    first, second = {}, {}
                    cut = True
                plus.wait_recv()
                r1 = region({axis: before, **first})
                on1 = go(r1.at[pl.ds(0, 2)] if cut else r1, axis, 1)
                minus.wait_recv()
                r2 = region({axis: after, **second})
                on2 = go(r2.at[pl.ds(2, 2)] if cut else r2, axis, 3)
                yield
                on1.wait_recv()
                on2.wait_recv()
            have[axis] = True

    chains = [chain(c) for c in range(4)]

    def low_copy(slot, owner, to):
        return pltpu.make_async_remote_copy(
            src_ref=low_all.at[owner], dst_ref=low_all.at[owner],
            send_sem=m_send.at[slot], recv_sem=m_recv.at[slot], device_id=(to, vert), device_id_type=MESH,
        )

    sibling = (ka // 2) * 2 + (ka + 1) % 2
    across = (ka + 2) % 4
    moves = []
    for c in range(4):
        for copy in exchanges[c]:
            copy.wait_recv()
        next(chains[c])
    for c in (2, 3, 0, 1):
        next(chains[c])
    take(low_recv.at[:, pl.ds(0, 7)], r2.at[1])
    lax.fori_loop(0, 32, arrange_low, 0)
    lax.fori_loop(1, 32, spread_low, 0)
    low_all[ka, vert] = stage_low[vert]
    for c in (2, 3, 0, 1):
        next(chains[c])
    take(low_all.at[0, pl.ds(0, 31)], l_recv)
    moves.append(low_copy(0, ka, sibling))
    moves.append(low_copy(1, ka, across))
    for m in moves:
        m.start()
    for c in (2, 3, 0, 1):
        next(chains[c])
    for c in (2, 3, 0, 1):
        next(chains[c])
    moves[1].wait_recv()
    moves.append(low_copy(2, across, sibling))
    moves[2].start()
    live_chains = [2, 3, 0, 1]
    while live_chains:
        for c in list(live_chains):
            if next(chains[c], "end") == "end":
                live_chains.remove(c)
    moves[0].wait_recv()
    moves[2].wait_recv()
    for c in dips:
        c.wait()

    def factor(k, d):
        return rot_ref[d, k] * coup_ref[d, k].astype(F32)

    def step(g, _):
        y, x = g // 2, g % 2
        sums = []
        for n in range(3):
            total = None
            for c in range(4):
                rows = uppers[c][y, x].reshape(256, WIDTHS[c])
                term = lax.dot_general(
                    rows, dip[n, :, STARTS[c]:STARTS[c] + WIDTHS[c]], NT, preferred_element_type=F32
                )
                total = term if total is None else total + term
            sums.append(total.reshape(4, 8, 8, 256))
        zero, up, down = sums
        rows = pl.ds(pl.multiple_of(g * 32, 32), 32)
        for k in range(8):
            value = factor(k, 0) * zero[:, k]
            if k < 7:
                value = value + factor(k, 1) * up[:, k + 1]
            if k > 0:
                value = value + factor(k, 2) * down[:, k - 1]
            half[rows, k * 256:(k + 1) * 256] = value.reshape(32, 256).astype(BF16)
        return 0

    lax.fori_loop(0, 8, step, 0)

    for t in range(4):
        total = None
        for o in range(4):
            lows = low_all[o, pl.ds(t * 8, 8)].reshape(128, 512)
            term = lax.dot_general(half[:, o * 512:(o + 1) * 512], lows, NT, preferred_element_type=F32)
            total = term if total is None else total + term
        tiles = total.reshape(32, 8, 128)
        for j in range(32):
            amp[(j // 8) * 4 + j % 4, t * 2 + (j // 4) % 2] = tiles[j]

    for k in range(1, 16):
        w = (plane + k) % 16
        send(amp.at[w], part1.at[plane], s1.at[2], r1.at[2], in_plane(w))
    part1[plane] = amp[plane]
    take(part1.at[pl.ds(0, 15)], r1.at[2])
    row_sum[...] = jnp.sum(part1[...], axis=0)
    for k in range(1, 8):
        p = (row + k) % 8
        send(row_sum.at[p], part2.at[row], s2.at[2], r2.at[2], in_row(p))
    part2[row] = row_sum[row]
    take(part2.at[pl.ds(0, 7)], r2.at[2])
    total = jnp.sum(part2[...], axis=0)
    out_ref[...] = total * total

    take(up_send.at[pl.ds(0, 7)], s1.at[0])
    take(up_recv.at[pl.ds(0, 15)], s2.at[0])
    take(low_send.at[pl.ds(0, 15)], s1.at[1])
    take(low_recv.at[:, pl.ds(0, 7)], s2.at[1])
    for copies in exchanges:
        for copy in copies:
            copy.wait_send()
    take(stage_low.at[pl.ds(0, 31)], l_send)
    for copy in sent + moves:
        copy.wait_send()
    take(amp.at[pl.ds(0, 15)], s1.at[2])
    take(row_sum.at[pl.ds(0, 7)], s2.at[2])


def per_device(
    eig_lower, eig_upper, layout_map, block_live, coupling, rot_coef, dip_zero, dip_raise, dip_lower
):
    heads = layout_map.reshape(512, 128)[:, 0] // 128
    hits = heads[None, :] == jnp.arange(512, dtype=jnp.int32)[:, None]
    device = jnp.arange(512, dtype=jnp.int32) // 4
    place = ((device // 8) % 4 * 4 + device % 4) * 8 + device // 32 * 2 + device // 4 % 2
    source = jnp.sum(jnp.where(hits, place[None, :], 0), axis=1)
    smem = pl.BlockSpec(memory_space=pltpu.SMEM)
    vmem = pl.BlockSpec(memory_space=pltpu.VMEM)
    hbm = pl.BlockSpec(memory_space=pl.ANY)
    dma = pltpu.SemaphoreType.DMA
    out = pl.pallas_call(
        kernel,
        out_shape=jax.ShapeDtypeStruct((8, 128), F32),
        in_specs=[smem] * 5 + [hbm] * 5,
        out_specs=vmem,
        scratch_shapes=[
            pltpu.VMEM((64, 8, 512), BF16),
            pltpu.VMEM((32, 8, 512), BF16),
            pltpu.VMEM((8, 16, 8, 128), BF16),
            pltpu.VMEM((8, 16, 8, 128), BF16),
            pltpu.VMEM((16, 8, 8, 128), BF16),
            pltpu.VMEM((16, 8, 2, 8, 128), BF16),
            pltpu.VMEM((16, 8, 2, 8, 128), BF16),
            pltpu.VMEM((16, 8, 2, 8, 128), BF16),
            *[pltpu.VMEM((4, 16, w), BF16) for w in WIDTHS],
            *[pltpu.VMEM((4, 2, 4, 4, 16, w), BF16) for w in WIDTHS],
            pltpu.VMEM((32, 16, 512), BF16),
            pltpu.VMEM((4, 32, 16, 512), BF16),
            pltpu.VMEM((3, 256, 2048), BF16),
            pltpu.VMEM((256, 2048), BF16),
            pltpu.VMEM((16, 8, 8, 128), F32),
            pltpu.VMEM((16, 8, 8, 128), F32),
            pltpu.VMEM((8, 8, 128), F32),
            pltpu.VMEM((8, 8, 128), F32),
            pltpu.SemaphoreType.REGULAR,
            dma((2,)), dma((3,)),
            dma((3,)), dma((3,)), dma((3,)), dma((3,)),
            dma((4, 3)), dma((4, 3)),
            dma((4, 9)), dma((4, 9)),
            dma, dma,
            dma((3,)), dma((3,)),
        ],
        compiler_params=pltpu.CompilerParams(
            collective_id=0, has_side_effects=True, vmem_limit_bytes=60 * 1024 * 1024
        ),
        cost_estimate=pl.CostEstimate(flops=7_000_000_000, bytes_accessed=5_000_000, transcendentals=0),
    )(
        heads, source, block_live, coupling.T, rot_coef.T,
        eig_lower.reshape(64, 8, 512), eig_upper.reshape(32, 8, 512), dip_zero, dip_raise, dip_lower,
    )
    return out.T


def solution(mesh):
    return jax.shard_map(
        per_device,
        mesh=mesh,
        in_specs=(
            P(None, ("ka", "vert")),
            P(None, ("ka", "vert")),
            P(),
            P(),
            P(),
            P(),
            P("vert", "ka"),
            P("vert", "ka"),
            P("vert", "ka"),
        ),
        out_specs=P("ka", "vert"),
        check_vma=False,
    )
```

```python
import jax
import jax.numpy as jnp
from jax import lax
from jax.experimental import pallas as pl
from jax.experimental.pallas import tpu as pltpu
from jax.sharding import PartitionSpec as P

F32 = jnp.float32
BF16 = jnp.bfloat16
MESH = pl.DeviceIdType.MESH
WIDTHS = (768, 768, 256, 256)
STARTS = (0, 768, 1536, 1792)
ORDERS = ("xyz", "xzy", "yzx", "zyx")
NT = (((1,), (1,)), ((), ()))


def kernel(
    head_ref, src_ref, live_ref, coup_ref, rot_ref, low_hbm, up_hbm, dz_hbm, dr_hbm, dl_hbm,
    out_ref,
    low_ref, up_ref, up_send, up_mid, up_recv, low_send, low_mid, low_recv,
    sta, stb, stc, std_, ua, ub, uc, ud, stage_low, low_all, dip, acc, half, amp, pair, part,
    ready, in_sem, dip_sem, s1, r1, s2, r2, q_send, q_recv, g_send, g_recv, l_send, l_recv, m_send, m_recv,
):
    ka = lax.axis_index("ka")
    vert = lax.axis_index("vert")
    yy = vert // 8
    xx = (vert // 4) % 2
    zz = vert % 4
    row = ka * 2 + xx
    plane = yy * 4 + zz
    stages = (sta, stb, stc, std_)
    uppers = (ua, ub, uc, ud)

    def in_row(p):
        return p // 2, yy * 8 + (p % 2) * 4 + zz

    def in_plane(w):
        return ka, (w // 4) * 8 + xx * 4 + w % 4

    def say(sem, to):
        pl.semaphore_signal(sem, inc=1, device_id=to, device_id_type=MESH)

    def take(ref, sem):
        pltpu.make_async_copy(ref, ref, sem).wait()

    def send(src, dst, out_sem, in_sem_, to):
        copy = pltpu.make_async_remote_copy(
            src_ref=src, dst_ref=dst, send_sem=out_sem, recv_sem=in_sem_, device_id=to, device_id_type=MESH
        )
        copy.start()
        return copy

    barrier = pltpu.get_barrier_semaphore()
    for k in range(1, 8):
        say(barrier, in_row((row + k) % 8))
    for k in range(1, 4):
        say(barrier, in_plane(((yy + k) % 4) * 4 + zz))
        say(barrier, in_plane(yy * 4 + (zz + k) % 4))
    loads = [pltpu.make_async_copy(h, v, in_sem.at[n]) for n, (h, v) in enumerate(((up_hbm, up_ref), (low_hbm, low_ref)))]
    dips = [pltpu.make_async_copy(h, dip.at[n], dip_sem.at[n]) for n, h in enumerate((dz_hbm, dr_hbm, dl_hbm))]
    for c in loads + dips:
        c.start()
    for c in loads:
        c.wait()

    lane = lax.broadcasted_iota(jnp.int32, (8, 128), 1)
    zeros = jnp.zeros((8, 128), jnp.int32)
    heads = [zeros + head_ref[(ka * 32 + vert) * 4 + r] for r in range(4)]
    owned = [[(heads[r] >= o * 128) & (heads[r] < (o + 1) * 128) for r in range(3)] for o in range(4)]

    def pack(j, _):
        x2, w2 = (j // 4) % 2, (j // 8) * 4 + j % 4
        for u in range(3):
            unit = up_ref[j] if u == 0 else low_ref[2 * j + u - 1]
            runs = [unit[:, r * 128:(r + 1) * 128].astype(F32) for r in range(4)]
            for o in range(4):
                value = runs[3]
                for r in range(3):
                    value = jnp.where(owned[o][r], runs[r], value)
                if u == 0:
                    up_send[o * 2 + x2, w2] = value.astype(BF16)
                else:
                    low_send[w2, o * 2 + x2, u - 1] = value.astype(BF16)
        return 0

    lax.fori_loop(0, 32, pack, 0)

    def clear(y, _):
        for n in range(3):
            acc[n, y] = jnp.zeros((2, 4, 64, 256), F32)
        return 0

    lax.fori_loop(0, 4, clear, 0)
    pl.semaphore_wait(barrier, 13)

    for k in range(1, 8):
        p = (row + k) % 8
        send(up_send.at[p], up_mid.at[row], s1.at[0], r1.at[0], in_row(p))
    for k in range(1, 4):
        say(ready, in_plane(yy * 4 + (zz + k) % 4))
    up_mid[row] = up_send[row]
    pl.semaphore_wait(ready, 3)
    for k in range(1, 16):
        w = (plane + k) % 16
        send(low_send.at[w], low_mid.at[plane], s1.at[1], r1.at[1], in_plane(w))
    take(up_mid.at[pl.ds(0, 7)], r1.at[0])
    for k in range(1, 16):
        w = (plane + k) % 16
        send(up_mid.at[:, w], up_recv.at[plane], s2.at[0], r2.at[0], in_plane(w))
    up_recv[plane] = up_mid[:, plane]
    low_mid[plane] = low_send[plane]
    take(up_recv.at[pl.ds(0, 15)], r2.at[0])

    lives = [live_ref[2 * ka + b] for b in range(2)]

    def arrange_up(q, _):
        for n in range(16):
            block = q * 16 + n
            halves = []
            for b in range(2):
                s = src_ref[ka * 128 + b * 64 + block]
                tile = up_recv[s // 8, s % 8].astype(F32)
                halves.append(jnp.where(lane + block * 128 < lives[b], tile, 0.0))
            both = jnp.concatenate(halves, axis=0).astype(BF16)
            for c in range(4):
                if STARTS[c] <= n * 128 < STARTS[c] + WIDTHS[c]:
                    at = n * 128 - STARTS[c]
                    stages[c][q, :, at:at + 128] = both
        return 0

    lax.fori_loop(0, 4, arrange_up, 0)

    exchanges = []
    for c in range(4):
        copies = []
        for d in range(1, 4):
            q = (ka + d) % 4
            copies.append(send(
                stages[c].at[q], uppers[c].at[yy, xx, zz, ka], q_send.at[c, d - 1], q_recv.at[c, d - 1], (q, vert)
            ))
        exchanges.append(copies)
        uppers[c][yy, xx, zz, ka] = stages[c][ka]

    def arrange_low(v, _):
        for b in range(2):
            for h in range(2):
                block = 2 * v + h
                s = src_ref[ka * 128 + b * 64 + block]
                keep = lane + block * 128 < lives[b]
                both = jnp.concatenate(
                    [jnp.where(keep, low_recv[s // 8, s % 8, u].astype(F32), 0.0) for u in range(2)], axis=0
                ).astype(BF16)
                at = b * 256 + h * 128
                stage_low[v, :, at:at + 128] = both
        return 0

    def spread_low(k, _):
        v2 = (vert + k) % 32
        send(stage_low.at[v2], low_all.at[ka, vert], l_send, l_recv, (ka, v2))
        return 0

    def vid(y, x, z):
        return y * 8 + x * 4 + z

    sent = []

    where = {"y": yy, "x": xx, "z": zz}
    sizes = {"y": 4, "x": 2, "z": 4}

    def chain(c):
        u = uppers[c]
        first, second, last = ORDERS[c]
        done = []
        count = 0

        def region(fixed, have):
            idx = []
            for name in "yxz":
                if name in fixed:
                    idx.append(fixed[name])
                elif name in have:
                    idx.append(pl.ds(0, sizes[name]))
                else:
                    idx.append(where[name])
            return u.at[tuple(idx)]

        def go(ref, axis, step):
            nonlocal count
            to = dict(where)
            to[axis] = (where[axis] + step) % sizes[axis]
            copy = send(
                ref, ref, g_send.at[c, count], g_recv.at[c, count], (ka, vid(to["y"], to["x"], to["z"]))
            )
            count += 1
            sent.append(copy)
            return copy

        def both(axis, fixed, have):
            ref = region(fixed, have)
            if axis == "x":
                return [go(ref, axis, 1)]
            return [go(ref, axis, 1), go(ref, axis, 3)]

        def onward(pair, axis, fixed, have, cut):
            before, after = (where[axis] + 3) % 4, (where[axis] + 1) % 4
            halves = ({}, {})
            if cut == "x":
                halves = ({"x": 0}, {"x": 1})
            elif cut in ("y", "z"):
                halves = ({cut: pl.ds(0, 2)}, {cut: pl.ds(2, 2)})
            out = []
            for side, (copy, came, step) in enumerate(((pair[0], before, 1), (pair[1], after, 3))):
                copy.wait_recv()
                ref = region({**fixed, axis: came, **halves[side]}, have)
                if cut == "o":
                    ref = ref.at[pl.ds(2 * side, 2)]
                out.append(go(ref, axis, step))
            return out

        begun = both(first, {}, "")
        yield
        if first == "x":
            begun[0].wait_recv()
        else:
            on = onward(begun, first, {}, "", "o")
            yield
            for copy in on:
                copy.wait_recv()
        cut = first
        here = where[second]
        middle = both(second, {}, first)
        batches = [({second: here}, both(last, {}, first))]
        yield
        on = onward(middle, second, {}, first, cut)
        for step in (3, 1):
            at = {second: (here + step) % 4}
            batches.append((at, both(last, at, first)))
        yield
        for copy in on:
            copy.wait_recv()
        at = {second: (here + 2) % 4}
        batches.append((at, both(last, at, first)))
        yield
        if last == "x":
            for _, copies in batches:
                copies[0].wait_recv()
            yield
            return
        ends = []
        for group in (batches[:1], batches[1:3], batches[3:]):
            for at, copies in group:
                ends.extend(onward(copies, last, at, first, "x"))
            yield
        for copy in ends:
            copy.wait_recv()
        yield

    chains = [chain(c) for c in range(4)]

    def run(*names):
        for c in names:
            next(chains[c])

    def low_copy(slot, owner, to):
        return pltpu.make_async_remote_copy(
            src_ref=low_all.at[owner], dst_ref=low_all.at[owner],
            send_sem=m_send.at[slot], recv_sem=m_recv.at[slot], device_id=(to, vert), device_id_type=MESH,
        )

    sibling = (ka // 2) * 2 + (ka + 1) % 2
    across = (ka + 2) % 4
    moves = []
    def term(c, n, rows):
        flat = rows.reshape(-1, WIDTHS[c])
        value = lax.dot_general(
            flat, dip[n, :, STARTS[c]:STARTS[c] + WIDTHS[c]], NT, preferred_element_type=F32
        )
        return value

    def add_z(z):
        def body(n, _):
            acc[n, :, :, z] += term(0, n, ua[:, :, z]).reshape(4, 2, 64, 256)
            return 0

        lax.fori_loop(0, 3, body, 0)

    def add_y(y):
        def body(n, _):
            acc[n, y] += term(1, n, ub[y]).reshape(2, 4, 64, 256)
            return 0

        lax.fori_loop(0, 3, body, 0)

    def add_x(x):
        def body(n, _):
            acc[n, :, x] += (term(2, n, uc[:, x]) + term(3, n, ud[:, x])).reshape(4, 4, 64, 256)
            return 0

        lax.fori_loop(0, 3, body, 0)

    for c in (2, 3, 0, 1):
        for copy in exchanges[c]:
            copy.wait_recv()
        run(c)
    run(2, 3)
    run(0, 1)
    take(low_mid.at[pl.ds(0, 15)], r1.at[1])
    for k in range(1, 8):
        p = (row + k) % 8
        send(low_mid.at[:, p], low_recv.at[:, row], s2.at[1], r2.at[1], in_row(p))
    low_recv[:, row] = low_mid[:, row]
    run(2, 3)
    run(0, 1)
    take(low_recv.at[:, pl.ds(0, 7)], r2.at[1])
    lax.fori_loop(0, 32, arrange_low, 0)
    lax.fori_loop(1, 32, spread_low, 0)
    low_all[ka, vert] = stage_low[vert]
    run(2, 3)
    run(0, 1)
    run(0, 1)
    run(2, 3)
    for c in dips:
        c.wait()
    take(low_all.at[0, pl.ds(0, 31)], l_recv)
    moves.append(low_copy(0, ka, sibling))
    moves.append(low_copy(1, ka, across))
    for m in moves:
        m.start()
    run(0, 1)
    add_z(zz)
    add_y(yy)
    run(0, 1)

    def sides(k, _):
        add_z((zz + 3 - 2 * k) % 4)
        add_y((yy + 3 - 2 * k) % 4)
        return 0

    lax.fori_loop(0, 2, sides, 0)
    add_x(xx)
    moves[1].wait_recv()
    moves.append(low_copy(2, across, sibling))
    moves[2].start()
    run(2, 3)
    add_x(1 - xx)
    run(0)
    add_z((zz + 2) % 4)
    run(1)
    add_y((yy + 2) % 4)
    moves[0].wait_recv()
    moves[2].wait_recv()

    def factor(k, d):
        return rot_ref[d, k] * coup_ref[d, k].astype(F32)

    def step(g, _):
        y, x = g // 2, g % 2
        sums = [acc[n, y, x].reshape(4, 8, 8, 256) for n in range(3)]
        zero, up, down = sums
        rows = pl.ds(pl.multiple_of(g * 32, 32), 32)
        for k in range(8):
            value = factor(k, 0) * zero[:, k]
            if k < 7:
                value = value + factor(k, 1) * up[:, k + 1]
            if k > 0:
                value = value + factor(k, 2) * down[:, k - 1]
            half[rows, k * 256:(k + 1) * 256] = value.reshape(32, 256).astype(BF16)
        return 0

    lax.fori_loop(0, 8, step, 0)

    for t in range(4):
        total = None
        for o in range(4):
            lows = low_all[o, pl.ds(t * 8, 8)].reshape(128, 512)
            term = lax.dot_general(half[:, o * 512:(o + 1) * 512], lows, NT, preferred_element_type=F32)
            total = term if total is None else total + term
        tiles = total.reshape(32, 8, 128)
        amp[t % 2, t // 2] = tiles

    core, side = ka % 2, ka // 2
    to_pair = send(amp.at[1 - core], pair, s1.at[2], r1.at[2], (sibling, vert))
    to_pair.wait_recv()
    pair[...] = pair[...] + amp[core]
    mine = side * 32 + vert

    def give(k, _):
        h2, v2 = (side + k // 32) % 2, (vert + k % 32) % 32
        send(pair.at[h2, v2], part.at[mine], s2.at[2], r2.at[2], (h2 * 2 + core, v2))
        return 0

    lax.fori_loop(1, 64, give, 0)
    part[mine] = pair[side, vert]
    take(part.at[pl.ds(0, 63)], r2.at[2])
    total = jnp.sum(part[...], axis=0)
    out_ref[...] = total * total

    take(up_send.at[pl.ds(0, 7)], s1.at[0])
    take(up_recv.at[pl.ds(0, 15)], s2.at[0])
    take(low_send.at[pl.ds(0, 15)], s1.at[1])
    take(low_recv.at[:, pl.ds(0, 7)], s2.at[1])
    for copies in exchanges:
        for copy in copies:
            copy.wait_send()
    take(stage_low.at[pl.ds(0, 31)], l_send)
    for copy in sent + moves:
        copy.wait_send()
    to_pair.wait_send()
    take(part.at[pl.ds(0, 63)], s2.at[2])


def per_device(
    eig_lower, eig_upper, layout_map, block_live, coupling, rot_coef, dip_zero, dip_raise, dip_lower
):
    heads = layout_map.reshape(512, 128)[:, 0] // 128
    hits = heads[None, :] == jnp.arange(512, dtype=jnp.int32)[:, None]
    device = jnp.arange(512, dtype=jnp.int32) // 4
    place = ((device // 8) % 4 * 4 + device % 4) * 8 + device // 32 * 2 + device // 4 % 2
    source = jnp.sum(jnp.where(hits, place[None, :], 0), axis=1)
    smem = pl.BlockSpec(memory_space=pltpu.SMEM)
    vmem = pl.BlockSpec(memory_space=pltpu.VMEM)
    hbm = pl.BlockSpec(memory_space=pl.ANY)
    dma = pltpu.SemaphoreType.DMA
    out = pl.pallas_call(
        kernel,
        out_shape=jax.ShapeDtypeStruct((8, 128), F32),
        in_specs=[smem] * 5 + [hbm] * 5,
        out_specs=vmem,
        scratch_shapes=[
            pltpu.VMEM((64, 8, 512), BF16),
            pltpu.VMEM((32, 8, 512), BF16),
            pltpu.VMEM((8, 16, 8, 128), BF16),
            pltpu.VMEM((8, 16, 8, 128), BF16),
            pltpu.VMEM((16, 8, 8, 128), BF16),
            pltpu.VMEM((16, 8, 2, 8, 128), BF16),
            pltpu.VMEM((16, 8, 2, 8, 128), BF16),
            pltpu.VMEM((16, 8, 2, 8, 128), BF16),
            *[pltpu.VMEM((4, 16, w), BF16) for w in WIDTHS],
            *[pltpu.VMEM((4, 2, 4, 4, 16, w), BF16) for w in WIDTHS],
            pltpu.VMEM((32, 16, 512), BF16),
            pltpu.VMEM((4, 32, 16, 512), BF16),
            pltpu.VMEM((3, 256, 2048), BF16),
            pltpu.VMEM((3, 4, 2, 4, 64, 256), F32),
            pltpu.VMEM((256, 2048), BF16),
            pltpu.VMEM((2, 2, 32, 8, 128), F32),
            pltpu.VMEM((2, 32, 8, 128), F32),
            pltpu.VMEM((64, 8, 128), F32),
            pltpu.SemaphoreType.REGULAR,
            dma((2,)), dma((3,)),
            dma((3,)), dma((3,)), dma((3,)), dma((3,)),
            dma((4, 3)), dma((4, 3)),
            dma((4, 24)), dma((4, 24)),
            dma, dma,
            dma((3,)), dma((3,)),
        ],
        compiler_params=pltpu.CompilerParams(
            collective_id=0, has_side_effects=True, vmem_limit_bytes=60 * 1024 * 1024
        ),
        cost_estimate=pl.CostEstimate(flops=7_000_000_000, bytes_accessed=5_000_000, transcendentals=0),
    )(
        heads, source, block_live, coupling.T, rot_coef.T,
        eig_lower.reshape(64, 8, 512), eig_upper.reshape(32, 8, 512), dip_zero, dip_raise, dip_lower,
    )
    return out.T


def solution(mesh):
    return jax.shard_map(
        per_device,
        mesh=mesh,
        in_specs=(
            P(None, ("ka", "vert")),
            P(None, ("ka", "vert")),
            P(),
            P(),
            P(),
            P(),
            P("vert", "ka"),
            P("vert", "ka"),
            P("vert", "ka"),
        ),
        out_specs=P("ka", "vert"),
        check_vma=False,
    )
```

```python
import jax
import jax.numpy as jnp
from jax import lax
from jax.experimental import pallas as pl
from jax.experimental.pallas import tpu as pltpu
from jax.sharding import PartitionSpec as P

F32 = jnp.float32
BF16 = jnp.bfloat16
MESH = pl.DeviceIdType.MESH
WIDTHS = (768, 768, 256, 256)
STARTS = (0, 768, 1536, 1792)
ORDERS = ("xyz", "xzy", "yzx", "zyx")
NT = (((1,), (1,)), ((), ()))


def kernel(
    head_ref, src_ref, live_ref, coup_ref, rot_ref, low_hbm, up_hbm, dz_hbm, dr_hbm, dl_hbm,
    out_ref,
    low_ref, up_ref, up_send, up_recv, low_send, low_mid, low_recv,
    sta, stb, stc, std_, ua, ub, uc, ud, stage_low, low_plane, low_all, dip, acc, half, amp, pair, part,
    ready, in_sem, dip_sem, s1, r1, s2, r2, q_send, q_recv, g_send, g_recv, l_send, l_recv, m_send, m_recv,
):
    ka = lax.axis_index("ka")
    vert = lax.axis_index("vert")
    yy = vert // 8
    xx = (vert // 4) % 2
    zz = vert % 4
    row = ka * 2 + xx
    plane = yy * 4 + zz
    stages = (sta, stb, stc, std_)
    uppers = (ua, ub, uc, ud)

    def in_row(p):
        return p // 2, yy * 8 + (p % 2) * 4 + zz

    def in_plane(w):
        return ka, (w // 4) * 8 + xx * 4 + w % 4

    def say(sem, to):
        pl.semaphore_signal(sem, inc=1, device_id=to, device_id_type=MESH)

    def take(ref, sem):
        pltpu.make_async_copy(ref, ref, sem).wait()

    def send(src, dst, out_sem, in_sem_, to):
        copy = pltpu.make_async_remote_copy(
            src_ref=src, dst_ref=dst, send_sem=out_sem, recv_sem=in_sem_, device_id=to, device_id_type=MESH
        )
        copy.start()
        return copy

    barrier = pltpu.get_barrier_semaphore()
    for k in range(1, 8):
        say(barrier, in_row((row + k) % 8))
    for k in range(1, 16):
        say(barrier, in_plane((plane + k) % 16))
    loads = [pltpu.make_async_copy(h, v, in_sem.at[n]) for n, (h, v) in enumerate(((up_hbm, up_ref), (low_hbm, low_ref)))]
    dips = [pltpu.make_async_copy(h, dip.at[n], dip_sem.at[n]) for n, h in enumerate((dz_hbm, dr_hbm, dl_hbm))]
    for c in loads + dips:
        c.start()
    for c in loads:
        c.wait()

    lane = lax.broadcasted_iota(jnp.int32, (8, 128), 1)
    zeros = jnp.zeros((8, 128), jnp.int32)
    heads = [zeros + head_ref[(ka * 32 + vert) * 4 + r] for r in range(4)]
    owned = [[(heads[r] >= o * 128) & (heads[r] < (o + 1) * 128) for r in range(3)] for o in range(4)]

    def pack(j, _):
        x2, w2 = (j // 4) % 2, (j // 8) * 4 + j % 4
        for u in range(3):
            unit = up_ref[j] if u == 0 else low_ref[2 * j + u - 1]
            runs = [unit[:, r * 128:(r + 1) * 128].astype(F32) for r in range(4)]
            for o in range(4):
                value = runs[3]
                for r in range(3):
                    value = jnp.where(owned[o][r], runs[r], value)
                if u == 0:
                    up_send[w2 * 8 + o * 2 + x2] = value.astype(BF16)
                else:
                    low_send[w2, o * 2 + x2, u - 1] = value.astype(BF16)
        return 0

    lax.fori_loop(0, 32, pack, 0)

    def clear(y, _):
        for n in range(3):
            acc[n, y] = jnp.zeros((2, 4, 64, 256), F32)
        return 0

    lax.fori_loop(0, 4, clear, 0)
    pl.semaphore_wait(barrier, 22)

    def give_up(w, p):
        send(up_send.at[w * 8 + p], up_recv.at[plane * 8 + row], s1.at[0], r1.at[0], (p // 2, (w // 4) * 8 + (p % 2) * 4 + w % 4))

    for k in range(1, 8):
        say(ready, in_row((row + k) % 8))
    for k in range(1, 16):
        w = (plane + k) % 16
        send(low_send.at[w], low_mid.at[plane], s1.at[1], r1.at[1], in_plane(w))

    def give_plane(k, _):
        give_up((plane + k) % 16, row)
        return 0

    def give_row(k, _):
        give_up(plane, (row + k) % 8)
        return 0

    lax.fori_loop(1, 16, give_plane, 0)
    lax.fori_loop(1, 8, give_row, 0)
    pl.semaphore_wait(ready, 7)

    def give_rest(k, _):
        give_up((plane + 1 + k // 7) % 16, (row + 1 + k % 7) % 8)
        return 0

    lax.fori_loop(0, 105, give_rest, 0)
    up_recv[plane * 8 + row] = up_send[plane * 8 + row]
    low_mid[plane] = low_send[plane]
    take(low_mid.at[pl.ds(0, 15)], r1.at[1])
    for k in range(1, 8):
        p = (row + k) % 8
        send(low_mid.at[:, p], low_recv.at[:, row], s2.at[1], r2.at[1], in_row(p))
    low_recv[:, row] = low_mid[:, row]
    take(up_recv.at[pl.ds(0, 127)], r1.at[0])

    lives = [live_ref[2 * ka + b] for b in range(2)]

    def arrange_up(q, _):
        for n in range(16):
            block = q * 16 + n
            halves = []
            for b in range(2):
                s = src_ref[ka * 128 + b * 64 + block]
                tile = up_recv[s].astype(F32)
                halves.append(jnp.where(lane + block * 128 < lives[b], tile, 0.0))
            both = jnp.concatenate(halves, axis=0).astype(BF16)
            for c in range(4):
                if STARTS[c] <= n * 128 < STARTS[c] + WIDTHS[c]:
                    at = n * 128 - STARTS[c]
                    stages[c][q, :, at:at + 128] = both
        return 0

    lax.fori_loop(0, 4, arrange_up, 0)

    exchanges = []
    for c in range(4):
        copies = []
        for d in range(1, 4):
            q = (ka + d) % 4
            copies.append(send(
                stages[c].at[q], uppers[c].at[yy, xx, zz, ka], q_send.at[c, d - 1], q_recv.at[c, d - 1], (q, vert)
            ))
        exchanges.append(copies)
        uppers[c][yy, xx, zz, ka] = stages[c][ka]

    def arrange_low(v, _):
        for b in range(2):
            for h in range(2):
                block = 2 * v + h
                s = src_ref[ka * 128 + b * 64 + block]
                keep = lane + block * 128 < lives[b]
                both = jnp.concatenate(
                    [jnp.where(keep, low_recv[s // 8, s % 8, u].astype(F32), 0.0) for u in range(2)], axis=0
                ).astype(BF16)
                at = b * 256 + h * 128
                stage_low[(v // 8) * 4 + v % 4, (v // 4) % 2, :, at:at + 128] = both
        return 0

    take(low_recv.at[:, pl.ds(0, 7)], r2.at[1])
    lax.fori_loop(0, 32, arrange_low, 0)
    for k in range(1, 16):
        w = (plane + k) % 16
        send(stage_low.at[w], low_plane.at[plane], l_send, l_recv, in_plane(w))
    low_plane[plane] = stage_low[plane]

    def vid(y, x, z):
        return y * 8 + x * 4 + z

    sent = []

    where = {"y": yy, "x": xx, "z": zz}
    sizes = {"y": 4, "x": 2, "z": 4}

    def chain(c):
        u = uppers[c]
        first, second, last = ORDERS[c]
        done = []
        count = 0

        def region(fixed, have):
            idx = []
            for name in "yxz":
                if name in fixed:
                    idx.append(fixed[name])
                elif name in have:
                    idx.append(pl.ds(0, sizes[name]))
                else:
                    idx.append(where[name])
            return u.at[tuple(idx)]

        def go(ref, axis, step):
            nonlocal count
            to = dict(where)
            to[axis] = (where[axis] + step) % sizes[axis]
            copy = send(
                ref, ref, g_send.at[c, count], g_recv.at[c, count], (ka, vid(to["y"], to["x"], to["z"]))
            )
            count += 1
            sent.append(copy)
            return copy

        def both(axis, fixed, have):
            ref = region(fixed, have)
            if axis == "x":
                return [go(ref, axis, 1)]
            return [go(ref, axis, 1), go(ref, axis, 3)]

        def onward(pair, axis, fixed, have, cut):
            before, after = (where[axis] + 3) % 4, (where[axis] + 1) % 4
            halves = ({}, {})
            if cut == "x":
                halves = ({"x": 0}, {"x": 1})
            elif cut in ("y", "z"):
                halves = ({cut: pl.ds(0, 2)}, {cut: pl.ds(2, 2)})
            out = []
            for side, (copy, came, step) in enumerate(((pair[0], before, 1), (pair[1], after, 3))):
                copy.wait_recv()
                ref = region({**fixed, axis: came, **halves[side]}, have)
                if cut == "o":
                    ref = ref.at[pl.ds(2 * side, 2)]
                out.append(go(ref, axis, step))
            return out

        begun = both(first, {}, "")
        yield
        if first == "x":
            begun[0].wait_recv()
        else:
            on = onward(begun, first, {}, "", "o")
            yield
            for copy in on:
                copy.wait_recv()
        cut = first
        here = where[second]
        middle = both(second, {}, first)
        if last == "x":
            batches = both(last, {second: here}, first)
        yield
        on = onward(middle, second, {}, first, cut)
        if last == "x":
            for step in (3, 1):
                batches += both(last, {second: (here + step) % 4}, first)
        yield
        for copy in on:
            copy.wait_recv()
        if last == "x":
            batches += both(last, {second: (here + 2) % 4}, first)
            yield
            for copy in batches:
                copy.wait_recv()
            yield
            return
        ends = both(last, {}, first + second)
        yield
        ends = onward(ends, last, {}, first + second, second)
        yield
        for copy in ends:
            copy.wait_recv()
        yield

    chains = [chain(c) for c in range(4)]

    def run(*names):
        for c in names:
            next(chains[c])

    core, side = ka % 2, ka // 2
    sibling = side * 2 + 1 - core

    def low_out(slot, h, x):
        return send(
            low_plane.at[:, x], low_all.at[core, side, xx], m_send.at[slot], m_recv.at[slot],
            (h * 2 + core, yy * 8 + x * 4 + zz),
        )

    moves = []
    def term(c, n, rows):
        flat = rows.reshape(-1, WIDTHS[c])
        value = lax.dot_general(
            flat, dip[n, :, STARTS[c]:STARTS[c] + WIDTHS[c]], NT, preferred_element_type=F32
        )
        return value

    def add_z(z):
        def body(n, _):
            acc[n, :, :, z] += term(0, n, ua[:, :, z]).reshape(4, 2, 64, 256)
            return 0

        lax.fori_loop(0, 3, body, 0)

    def add_y(y):
        def body(n, _):
            acc[n, y] += term(1, n, ub[y]).reshape(2, 4, 64, 256)
            return 0

        lax.fori_loop(0, 3, body, 0)

    def add_x(x):
        def body(n, _):
            acc[n, :, x] += (term(2, n, uc[:, x]) + term(3, n, ud[:, x])).reshape(4, 4, 64, 256)
            return 0

        lax.fori_loop(0, 3, body, 0)

    for c in (2, 3, 0, 1):
        for copy in exchanges[c]:
            copy.wait_recv()
        run(c)
    run(2, 3)
    run(0, 1)
    run(2, 3)
    run(0, 1)
    take(low_plane.at[pl.ds(0, 15)], l_recv)
    moves.append(low_out(0, side, 1 - xx))
    moves.append(low_out(1, 1 - side, 1 - xx))
    moves.append(low_out(2, 1 - side, xx))
    low_all[core, side, xx] = low_plane[:, xx]
    run(2, 3)
    run(0, 1)
    run(2, 3)
    for c in dips:
        c.wait()
    add_z(zz)
    add_y(yy)
    add_x(xx)
    run(0, 1)

    def sides(k, _):
        add_z((zz + 3 - 2 * k) % 4)
        add_y((yy + 3 - 2 * k) % 4)
        return 0

    lax.fori_loop(0, 2, sides, 0)
    run(2, 3)
    add_x(1 - xx)
    for m in moves:
        m.wait_recv()
    moves.append(send(
        low_all.at[core], low_all.at[core], m_send.at[3], m_recv.at[3], (sibling, vert)
    ))
    run(0)
    add_z((zz + 2) % 4)
    run(1)
    add_y((yy + 2) % 4)
    moves[3].wait_recv()

    def factor(k, d):
        return rot_ref[d, k] * coup_ref[d, k].astype(F32)

    def step(g, _):
        y, x = g // 2, g % 2
        sums = [acc[n, y, x].reshape(4, 8, 8, 256) for n in range(3)]
        zero, up, down = sums
        rows = pl.ds(pl.multiple_of(g * 32, 32), 32)
        for k in range(8):
            value = factor(k, 0) * zero[:, k]
            if k < 7:
                value = value + factor(k, 1) * up[:, k + 1]
            if k > 0:
                value = value + factor(k, 2) * down[:, k - 1]
            half[rows, k * 256:(k + 1) * 256] = value.reshape(32, 256).astype(BF16)
        return 0

    lax.fori_loop(0, 8, step, 0)

    def amplitude(c, h):
        quarter = (h * 2 + c) * 4
        total = None
        for o in range(4):
            lows = low_all[o % 2, o // 2, :, pl.ds(quarter, 4)].reshape(128, 512)
            value = lax.dot_general(half[:, o * 512:(o + 1) * 512], lows, NT, preferred_element_type=F32)
            total = value if total is None else total + value
        amp[c, h] = total.reshape(32, 8, 128)

    def others(h, _):
        amplitude(1 - core, h)
        return 0

    def own(h, _):
        amplitude(core, h)
        return 0

    lax.fori_loop(0, 2, others, 0)
    to_pair = send(amp.at[1 - core], pair, s1.at[2], r1.at[2], (sibling, vert))
    lax.fori_loop(0, 2, own, 0)

    to_pair.wait_recv()
    pair[...] = pair[...] + amp[core]
    mine = side * 32 + vert

    def give(k, _):
        h2, v2 = (side + k // 32) % 2, (vert + k % 32) % 32
        send(pair.at[h2, v2], part.at[mine], s2.at[2], r2.at[2], (h2 * 2 + core, v2))
        return 0

    lax.fori_loop(1, 64, give, 0)
    part[mine] = pair[side, vert]
    take(part.at[pl.ds(0, 63)], r2.at[2])
    total = jnp.sum(part[...], axis=0)
    out_ref[...] = total * total

    take(up_send.at[pl.ds(0, 127)], s1.at[0])
    take(low_send.at[pl.ds(0, 15)], s1.at[1])
    take(low_recv.at[:, pl.ds(0, 7)], s2.at[1])
    for copies in exchanges:
        for copy in copies:
            copy.wait_send()
    take(stage_low.at[pl.ds(0, 15)], l_send)
    for copy in sent + moves:
        copy.wait_send()
    to_pair.wait_send()
    take(part.at[pl.ds(0, 63)], s2.at[2])


def per_device(
    eig_lower, eig_upper, layout_map, block_live, coupling, rot_coef, dip_zero, dip_raise, dip_lower
):
    heads = layout_map.reshape(512, 128)[:, 0] // 128
    hits = heads[None, :] == jnp.arange(512, dtype=jnp.int32)[:, None]
    device = jnp.arange(512, dtype=jnp.int32) // 4
    place = ((device // 8) % 4 * 4 + device % 4) * 8 + device // 32 * 2 + device // 4 % 2
    source = jnp.sum(jnp.where(hits, place[None, :], 0), axis=1)
    smem = pl.BlockSpec(memory_space=pltpu.SMEM)
    vmem = pl.BlockSpec(memory_space=pltpu.VMEM)
    hbm = pl.BlockSpec(memory_space=pl.ANY)
    dma = pltpu.SemaphoreType.DMA
    out = pl.pallas_call(
        kernel,
        out_shape=jax.ShapeDtypeStruct((8, 128), F32),
        in_specs=[smem] * 5 + [hbm] * 5,
        out_specs=vmem,
        scratch_shapes=[
            pltpu.VMEM((64, 8, 512), BF16),
            pltpu.VMEM((32, 8, 512), BF16),
            pltpu.VMEM((128, 8, 128), BF16),
            pltpu.VMEM((128, 8, 128), BF16),
            pltpu.VMEM((16, 8, 2, 8, 128), BF16),
            pltpu.VMEM((16, 8, 2, 8, 128), BF16),
            pltpu.VMEM((16, 8, 2, 8, 128), BF16),
            *[pltpu.VMEM((4, 16, w), BF16) for w in WIDTHS],
            *[pltpu.VMEM((4, 2, 4, 4, 16, w), BF16) for w in WIDTHS],
            pltpu.VMEM((16, 2, 16, 512), BF16),
            pltpu.VMEM((16, 2, 16, 512), BF16),
            pltpu.VMEM((2, 2, 2, 16, 16, 512), BF16),
            pltpu.VMEM((3, 256, 2048), BF16),
            pltpu.VMEM((3, 4, 2, 4, 64, 256), F32),
            pltpu.VMEM((256, 2048), BF16),
            pltpu.VMEM((2, 2, 32, 8, 128), F32),
            pltpu.VMEM((2, 32, 8, 128), F32),
            pltpu.VMEM((64, 8, 128), F32),
            pltpu.SemaphoreType.REGULAR,
            dma((2,)), dma((3,)),
            dma((3,)), dma((3,)), dma((3,)), dma((3,)),
            dma((4, 3)), dma((4, 3)),
            dma((4, 24)), dma((4, 24)),
            dma, dma,
            dma((4,)), dma((4,)),
        ],
        compiler_params=pltpu.CompilerParams(
            collective_id=0, has_side_effects=True, vmem_limit_bytes=60 * 1024 * 1024
        ),
        cost_estimate=pl.CostEstimate(flops=7_000_000_000, bytes_accessed=5_000_000, transcendentals=0),
    )(
        heads, source, block_live, coupling.T, rot_coef.T,
        eig_lower.reshape(64, 8, 512), eig_upper.reshape(32, 8, 512), dip_zero, dip_raise, dip_lower,
    )
    return out.T


def solution(mesh):
    return jax.shard_map(
        per_device,
        mesh=mesh,
        in_specs=(
            P(None, ("ka", "vert")),
            P(None, ("ka", "vert")),
            P(),
            P(),
            P(),
            P(),
            P("vert", "ka"),
            P("vert", "ka"),
            P("vert", "ka"),
        ),
        out_specs=P("ka", "vert"),
        check_vma=False,
    )
```

```python
import jax
import jax.numpy as jnp
from jax import lax
from jax.experimental import pallas as pl
from jax.experimental.pallas import tpu as pltpu
from jax.sharding import PartitionSpec as P

F32 = jnp.float32
BF16 = jnp.bfloat16
MESH = pl.DeviceIdType.MESH
WIDTHS = (512, 512, 256, 256, 256, 256)
STARTS = (0, 512, 1024, 1280, 1536, 1792)
ORDERS = ("xyz", "xzy", "yzx", "zyx", "xyz", "xzy")
CHAINS = len(WIDTHS)
NT = (((1,), (1,)), ((), ()))


def kernel(
    head_ref, src_ref, live_ref, coup_ref, rot_ref, low_hbm, up_hbm, dz_hbm, dr_hbm, dl_hbm,
    out_ref,
    low_ref, up_ref, up_send, up_recv, low_send, low_mid, low_recv,
    sta, stb, stc, std_, ste, stf, ua, ub, uc, ud, ue, uf, stage_low, low_plane, low_all, dip, acc, half, amp, pair, part,
    ready, in_sem, dip_sem, s1, r1, s2, r2, q_send, q_recv, g_send, g_recv, l_send, l_recv, m_send, m_recv,
):
    ka = lax.axis_index("ka")
    vert = lax.axis_index("vert")
    yy = vert // 8
    xx = (vert // 4) % 2
    zz = vert % 4
    row = ka * 2 + xx
    plane = yy * 4 + zz
    stages = (sta, stb, stc, std_, ste, stf)
    uppers = (ua, ub, uc, ud, ue, uf)

    def in_row(p):
        return p // 2, yy * 8 + (p % 2) * 4 + zz

    def in_plane(w):
        return ka, (w // 4) * 8 + xx * 4 + w % 4

    def say(sem, to):
        pl.semaphore_signal(sem, inc=1, device_id=to, device_id_type=MESH)

    def take(ref, sem):
        pltpu.make_async_copy(ref, ref, sem).wait()

    def send(src, dst, out_sem, in_sem_, to):
        copy = pltpu.make_async_remote_copy(
            src_ref=src, dst_ref=dst, send_sem=out_sem, recv_sem=in_sem_, device_id=to, device_id_type=MESH
        )
        copy.start()
        return copy

    barrier = pltpu.get_barrier_semaphore()
    def each(count, body):
        def step(k, _):
            body(k)
            return 0

        lax.fori_loop(1, count, step, 0)

    each(8, lambda k: say(barrier, in_row((row + k) % 8)))
    each(16, lambda k: say(barrier, in_plane((plane + k) % 16)))
    loads = [pltpu.make_async_copy(h, v, in_sem.at[n]) for n, (h, v) in enumerate(((up_hbm, up_ref), (low_hbm, low_ref)))]
    dips = [pltpu.make_async_copy(h, dip.at[n], dip_sem.at[n]) for n, h in enumerate((dz_hbm, dr_hbm, dl_hbm))]
    for c in loads + dips:
        c.start()
    for c in loads:
        c.wait()

    lane = lax.broadcasted_iota(jnp.int32, (8, 128), 1)
    zeros = jnp.zeros((8, 128), jnp.int32)
    heads = [zeros + head_ref[(ka * 32 + vert) * 4 + r] for r in range(4)]
    owned = [[(heads[r] >= o * 128) & (heads[r] < (o + 1) * 128) for r in range(3)] for o in range(4)]

    def pack(j, _):
        x2, w2 = (j // 4) % 2, (j // 8) * 4 + j % 4
        for u in range(3):
            unit = up_ref[j] if u == 0 else low_ref[2 * j + u - 1]
            runs = [unit[:, r * 128:(r + 1) * 128].astype(F32) for r in range(4)]
            for o in range(4):
                value = runs[3]
                for r in range(3):
                    value = jnp.where(owned[o][r], runs[r], value)
                if u == 0:
                    up_send[w2 * 8 + o * 2 + x2] = value.astype(BF16)
                else:
                    low_send[w2, o * 2 + x2, u - 1] = value.astype(BF16)
        return 0

    lax.fori_loop(0, 32, pack, 0)

    def clear(y, _):
        for n in range(3):
            acc[n, y] = jnp.zeros((2, 4, 64, 256), F32)
        return 0

    lax.fori_loop(0, 4, clear, 0)
    pl.semaphore_wait(barrier, 22)

    def give_up(w, p):
        send(up_send.at[w * 8 + p], up_recv.at[plane * 8 + row], s1.at[0], r1.at[0], (p // 2, (w // 4) * 8 + (p % 2) * 4 + w % 4))

    each(8, lambda k: say(ready, in_row((row + k) % 8)))

    def give_plane(k, _):
        give_up((plane + k) % 16, row)
        return 0

    def give_row(k, _):
        give_up(plane, (row + k) % 8)
        return 0

    lax.fori_loop(1, 16, give_plane, 0)
    lax.fori_loop(1, 8, give_row, 0)
    pl.semaphore_wait(ready, 7)

    def give_rest(k, _):
        give_up((plane + 1 + k // 7) % 16, (row + 1 + k % 7) % 8)
        return 0

    lax.fori_loop(0, 105, give_rest, 0)
    up_recv[plane * 8 + row] = up_send[plane * 8 + row]
    take(up_recv.at[pl.ds(0, 127)], r1.at[0])

    def give_mid(k):
        w = (plane + k) % 16
        send(low_send.at[w], low_mid.at[plane], s1.at[1], r1.at[1], in_plane(w))

    each(16, give_mid)
    low_mid[plane] = low_send[plane]

    lives = [live_ref[2 * ka + b] for b in range(2)]

    def arrange_up(q, _):
        for n in range(16):
            block = q * 16 + n
            halves = []
            for b in range(2):
                s = src_ref[ka * 128 + b * 64 + block]
                tile = up_recv[s].astype(F32)
                halves.append(jnp.where(lane + block * 128 < lives[b], tile, 0.0))
            both = jnp.concatenate(halves, axis=0).astype(BF16)
            for c in range(CHAINS):
                if STARTS[c] <= n * 128 < STARTS[c] + WIDTHS[c]:
                    at = n * 128 - STARTS[c]
                    stages[c][q, :, at:at + 128] = both
        return 0

    lax.fori_loop(0, 4, arrange_up, 0)

    order = (4, 5, 2, 3, 0, 1)

    for c in order:
        for d in range(1, 4):
            q = (ka + d) % 4
            send(
                stages[c].at[q], uppers[c].at[yy, xx, zz, ka], q_send.at[c], q_recv.at[c], (q, vert)
            )
        uppers[c][yy, xx, zz, ka] = stages[c][ka]

    def arrange_low(v, _):
        for b in range(2):
            for h in range(2):
                block = 2 * v + h
                s = src_ref[ka * 128 + b * 64 + block]
                keep = lane + block * 128 < lives[b]
                both = jnp.concatenate(
                    [jnp.where(keep, low_recv[s // 8, s % 8, u].astype(F32), 0.0) for u in range(2)], axis=0
                ).astype(BF16)
                at = b * 256 + h * 128
                stage_low[(v // 8) * 4 + v % 4, (v // 4) % 2, :, at:at + 128] = both
        return 0

    def vid(y, x, z):
        return y * 8 + x * 4 + z

    sent = []

    where = {"y": yy, "x": xx, "z": zz}
    sizes = {"y": 4, "x": 2, "z": 4}

    def chain(c):
        u = uppers[c]
        first, second, last = ORDERS[c]
        done = []
        count = 0

        def region(fixed, have):
            idx = []
            for name in "yxz":
                if name in fixed:
                    idx.append(fixed[name])
                elif name in have:
                    idx.append(pl.ds(0, sizes[name]))
                else:
                    idx.append(where[name])
            return u.at[tuple(idx)]

        def go(ref, axis, step):
            nonlocal count
            to = dict(where)
            to[axis] = (where[axis] + step) % sizes[axis]
            copy = send(
                ref, ref, g_send.at[c, count], g_recv.at[c, count], (ka, vid(to["y"], to["x"], to["z"]))
            )
            count += 1
            sent.append(copy)
            return copy

        def both(axis, fixed, have):
            ref = region(fixed, have)
            if axis == "x":
                return [go(ref, axis, 1)]
            return [go(ref, axis, 1), go(ref, axis, 3)]

        def onward(pair, axis, fixed, have, cut):
            before, after = (where[axis] + 3) % 4, (where[axis] + 1) % 4
            halves = ({}, {})
            if cut == "x":
                halves = ({"x": 0}, {"x": 1})
            elif cut in ("y", "z"):
                halves = ({cut: pl.ds(0, 2)}, {cut: pl.ds(2, 2)})
            out = []
            for side, (copy, came, step) in enumerate(((pair[0], before, 1), (pair[1], after, 3))):
                copy.wait_recv()
                ref = region({**fixed, axis: came, **halves[side]}, have)
                if cut == "o":
                    ref = ref.at[pl.ds(2 * side, 2)]
                out.append(go(ref, axis, step))
            return out

        begun = both(first, {}, "")
        yield
        if first == "x":
            begun[0].wait_recv()
        else:
            on = onward(begun, first, {}, "", "o")
            yield
            for copy in on:
                copy.wait_recv()
        cut = first
        here = where[second]
        middle = both(second, {}, first)
        if last == "x":
            batches = both(last, {second: here}, first)
        yield
        on = onward(middle, second, {}, first, cut)
        if last == "x":
            for step in (3, 1):
                batches += both(last, {second: (here + step) % 4}, first)
        yield
        for copy in on:
            copy.wait_recv()
        if last == "x":
            batches += both(last, {second: (here + 2) % 4}, first)
            yield
            for copy in batches:
                copy.wait_recv()
            yield
            return
        ends = both(last, {}, first + second)
        yield
        ends = onward(ends, last, {}, first + second, second)
        yield
        for copy in ends:
            copy.wait_recv()
        yield

    chains = [chain(c) for c in range(CHAINS)]

    def run(*names):
        for c in names:
            next(chains[c])

    core, side = ka % 2, ka // 2
    sibling = side * 2 + 1 - core

    def low_out(slot, h, x):
        return send(
            low_plane.at[:, x], low_all.at[core, side, xx], m_send.at[slot], m_recv.at[slot],
            (h * 2 + core, yy * 8 + x * 4 + zz),
        )

    moves = []
    def term(c, n, rows):
        flat = rows.reshape(-1, WIDTHS[c])
        value = lax.dot_general(
            flat, dip[n, :, STARTS[c]:STARTS[c] + WIDTHS[c]], NT, preferred_element_type=F32
        )
        return value

    def add_z(z):
        def body(n, _):
            acc[n, :, :, z] += (term(0, n, ua[:, :, z]) + term(4, n, ue[:, :, z])).reshape(4, 2, 64, 256)
            return 0

        lax.fori_loop(0, 3, body, 0)

    def add_y(y):
        def body(n, _):
            acc[n, y] += (term(1, n, ub[y]) + term(5, n, uf[y])).reshape(2, 4, 64, 256)
            return 0

        lax.fori_loop(0, 3, body, 0)

    def add_x(x):
        def body(n, _):
            acc[n, :, x] += (term(2, n, uc[:, x]) + term(3, n, ud[:, x])).reshape(4, 4, 64, 256)
            return 0

        lax.fori_loop(0, 3, body, 0)

    for c in order:
        take(stages[c].at[pl.ds(0, 3)], q_recv.at[c])
        run(c)
    run(4, 5)
    run(2, 3)
    run(0, 1)
    run(4, 5)
    take(low_mid.at[pl.ds(0, 15)], r1.at[1])

    def give_low(k):
        p = (row + k) % 8
        send(low_mid.at[:, p], low_recv.at[:, row], s2.at[1], r2.at[1], in_row(p))

    each(8, give_low)
    low_recv[:, row] = low_mid[:, row]
    run(2, 3)
    run(4, 5)
    run(0, 1)
    run(2, 3)
    run(0, 1)
    run(2, 3)
    take(low_recv.at[:, pl.ds(0, 7)], r2.at[1])
    lax.fori_loop(0, 32, arrange_low, 0)

    def give_rows(k):
        w = (plane + k) % 16
        send(stage_low.at[w], low_plane.at[plane], l_send, l_recv, in_plane(w))

    each(16, give_rows)
    low_plane[plane] = stage_low[plane]
    for c in dips:
        c.wait()
    add_z(zz)
    add_y(yy)
    run(4, 5)
    take(low_plane.at[pl.ds(0, 15)], l_recv)
    moves.append(low_out(0, side, 1 - xx))
    moves.append(low_out(1, 1 - side, 1 - xx))
    moves.append(low_out(2, 1 - side, xx))
    low_all[core, side, xx] = low_plane[:, xx]
    add_x(xx)
    run(0, 1)

    def sides(k, _):
        add_z((zz + 3 - 2 * k) % 4)
        add_y((yy + 3 - 2 * k) % 4)
        return 0

    lax.fori_loop(0, 2, sides, 0)
    run(2, 3)
    add_x(1 - xx)
    for m in moves:
        m.wait_recv()
    moves.append(send(
        low_all.at[core], low_all.at[core], m_send.at[3], m_recv.at[3], (sibling, vert)
    ))
    run(4, 0)
    add_z((zz + 2) % 4)
    run(5, 1)
    add_y((yy + 2) % 4)
    moves[3].wait_recv()

    def factor(k, d):
        return rot_ref[d, k] * coup_ref[d, k].astype(F32)

    def step(g, _):
        y, x = g // 2, g % 2
        sums = [acc[n, y, x].reshape(4, 8, 8, 256) for n in range(3)]
        zero, up, down = sums
        rows = pl.ds(pl.multiple_of(g * 32, 32), 32)
        for k in range(8):
            value = factor(k, 0) * zero[:, k]
            if k < 7:
                value = value + factor(k, 1) * up[:, k + 1]
            if k > 0:
                value = value + factor(k, 2) * down[:, k - 1]
            half[rows, k * 256:(k + 1) * 256] = value.reshape(32, 256).astype(BF16)
        return 0

    lax.fori_loop(0, 8, step, 0)

    def amplitude(c, h):
        quarter = (h * 2 + c) * 4
        total = None
        for o in range(4):
            lows = low_all[o % 2, o // 2, :, pl.ds(quarter, 4)].reshape(128, 512)
            value = lax.dot_general(half[:, o * 512:(o + 1) * 512], lows, NT, preferred_element_type=F32)
            total = value if total is None else total + value
        amp[c, h] = total.reshape(32, 8, 128)

    def others(h, _):
        amplitude(1 - core, h)
        return 0

    def own(h, _):
        amplitude(core, h)
        return 0

    lax.fori_loop(0, 2, others, 0)
    to_pair = send(amp.at[1 - core], pair, s1.at[2], r1.at[2], (sibling, vert))
    lax.fori_loop(0, 2, own, 0)

    to_pair.wait_recv()
    pair[...] = pair[...] + amp[core]
    mine = side * 32 + vert

    def give(k, _):
        h2, v2 = (side + k // 32) % 2, (vert + k % 32) % 32
        send(pair.at[h2, v2], part.at[mine], s2.at[2], r2.at[2], (h2 * 2 + core, v2))
        return 0

    lax.fori_loop(1, 64, give, 0)
    part[mine] = pair[side, vert]
    take(up_send.at[pl.ds(0, 127)], s1.at[0])
    take(low_send.at[pl.ds(0, 15)], s1.at[1])
    take(low_recv.at[:, pl.ds(0, 7)], s2.at[1])
    for c in order:
        take(stages[c].at[pl.ds(0, 3)], q_send.at[c])
    take(stage_low.at[pl.ds(0, 15)], l_send)
    for copy in sent + moves:
        copy.wait_send()
    to_pair.wait_send()
    take(part.at[pl.ds(0, 63)], s2.at[2])
    take(part.at[pl.ds(0, 63)], r2.at[2])
    total = jnp.sum(part[...], axis=0)
    out_ref[...] = total * total


def per_device(
    eig_lower, eig_upper, layout_map, block_live, coupling, rot_coef, dip_zero, dip_raise, dip_lower
):
    heads = layout_map.reshape(512, 128)[:, 0] // 128
    hits = heads[None, :] == jnp.arange(512, dtype=jnp.int32)[:, None]
    device = jnp.arange(512, dtype=jnp.int32) // 4
    place = ((device // 8) % 4 * 4 + device % 4) * 8 + device // 32 * 2 + device // 4 % 2
    source = jnp.sum(jnp.where(hits, place[None, :], 0), axis=1)
    smem = pl.BlockSpec(memory_space=pltpu.SMEM)
    vmem = pl.BlockSpec(memory_space=pltpu.VMEM)
    hbm = pl.BlockSpec(memory_space=pl.ANY)
    dma = pltpu.SemaphoreType.DMA
    out = pl.pallas_call(
        kernel,
        out_shape=jax.ShapeDtypeStruct((8, 128), F32),
        in_specs=[smem] * 5 + [hbm] * 5,
        out_specs=vmem,
        scratch_shapes=[
            pltpu.VMEM((64, 8, 512), BF16),
            pltpu.VMEM((32, 8, 512), BF16),
            pltpu.VMEM((128, 8, 128), BF16),
            pltpu.VMEM((128, 8, 128), BF16),
            pltpu.VMEM((16, 8, 2, 8, 128), BF16),
            pltpu.VMEM((16, 8, 2, 8, 128), BF16),
            pltpu.VMEM((16, 8, 2, 8, 128), BF16),
            *[pltpu.VMEM((4, 16, w), BF16) for w in WIDTHS],
            *[pltpu.VMEM((4, 2, 4, 4, 16, w), BF16) for w in WIDTHS],
            pltpu.VMEM((16, 2, 16, 512), BF16),
            pltpu.VMEM((16, 2, 16, 512), BF16),
            pltpu.VMEM((2, 2, 2, 16, 16, 512), BF16),
            pltpu.VMEM((3, 256, 2048), BF16),
            pltpu.VMEM((3, 4, 2, 4, 64, 256), F32),
            pltpu.VMEM((256, 2048), BF16),
            pltpu.VMEM((2, 2, 32, 8, 128), F32),
            pltpu.VMEM((2, 32, 8, 128), F32),
            pltpu.VMEM((64, 8, 128), F32),
            pltpu.SemaphoreType.REGULAR,
            dma((2,)), dma((3,)),
            dma((3,)), dma((3,)), dma((3,)), dma((3,)),
            dma((CHAINS,)), dma((CHAINS,)),
            dma((CHAINS, 12)), dma((CHAINS, 12)),
            dma, dma,
            dma((4,)), dma((4,)),
        ],
        compiler_params=pltpu.CompilerParams(
            collective_id=0, has_side_effects=True, vmem_limit_bytes=60 * 1024 * 1024
        ),
        cost_estimate=pl.CostEstimate(flops=7_000_000_000, bytes_accessed=5_000_000, transcendentals=0),
    )(
        heads, source, block_live, coupling.T, rot_coef.T,
        eig_lower.reshape(64, 8, 512), eig_upper.reshape(32, 8, 512), dip_zero, dip_raise, dip_lower,
    )
    return out.T


def solution(mesh):
    return jax.shard_map(
        per_device,
        mesh=mesh,
        in_specs=(
            P(None, ("ka", "vert")),
            P(None, ("ka", "vert")),
            P(),
            P(),
            P(),
            P(),
            P("vert", "ka"),
            P("vert", "ka"),
            P("vert", "ka"),
        ),
        out_specs=P("ka", "vert"),
        check_vma=False,
    )
```

```python
import jax
import jax.numpy as jnp
from jax import lax
from jax.experimental import pallas as pl
from jax.experimental.pallas import tpu as pltpu
from jax.sharding import PartitionSpec as P

F32 = jnp.float32
BF16 = jnp.bfloat16
MESH = pl.DeviceIdType.MESH
WIDTHS = (512, 512, 256, 256, 256, 256)
STARTS = (0, 512, 1024, 1280, 1536, 1792)
ORDERS = ("xyz", "xzy", "yzx", "zyx", "xyz", "xzy")
CHAINS = len(WIDTHS)
NT = (((1,), (1,)), ((), ()))


def kernel(
    live_ref, coup_ref, rot_ref, map_hbm, low_hbm, up_hbm, dz_hbm, dr_hbm, dl_hbm,
    out_ref,
    map_ref, table, src_ref, low_ref, up_ref, up_send, up_recv, low_send, low_mid, low_recv,
    sta, stb, stc, std_, ste, stf, ua, ub, uc, ud, ue, uf, stage_low, low_plane, low_all, dip, acc, half, amp, pair, part,
    ready, in_sem, dip_sem, s1, r1, s2, r2, q_send, q_recv, g_send, g_recv, l_send, l_recv, m_send, m_recv,
):
    ka = lax.axis_index("ka")
    vert = lax.axis_index("vert")
    yy = vert // 8
    xx = (vert // 4) % 2
    zz = vert % 4
    row = ka * 2 + xx
    plane = yy * 4 + zz
    stages = (sta, stb, stc, std_, ste, stf)
    uppers = (ua, ub, uc, ud, ue, uf)

    def in_row(p):
        return p // 2, yy * 8 + (p % 2) * 4 + zz

    def in_plane(w):
        return ka, (w // 4) * 8 + xx * 4 + w % 4

    def say(sem, to):
        pl.semaphore_signal(sem, inc=1, device_id=to, device_id_type=MESH)

    def take(ref, sem):
        pltpu.make_async_copy(ref, ref, sem).wait()

    def send(src, dst, out_sem, in_sem_, to):
        copy = pltpu.make_async_remote_copy(
            src_ref=src, dst_ref=dst, send_sem=out_sem, recv_sem=in_sem_, device_id=to, device_id_type=MESH
        )
        copy.start()
        return copy

    barrier = pltpu.get_barrier_semaphore()
    def each(count, body):
        def step(k, _):
            body(k)
            return 0

        lax.fori_loop(1, count, step, 0)

    each(8, lambda k: say(barrier, in_row((row + k) % 8)))
    each(16, lambda k: say(barrier, in_plane((plane + k) % 16)))
    loads = [pltpu.make_async_copy(h, v, in_sem.at[n]) for n, (h, v) in enumerate(((map_hbm, map_ref), (up_hbm, up_ref), (low_hbm, low_ref)))]
    dips = [pltpu.make_async_copy(h, dip.at[n], dip_sem.at[n]) for n, h in enumerate((dz_hbm, dr_hbm, dl_hbm))]
    for c in loads + dips:
        c.start()
    for c in loads:
        c.wait()

    lane = lax.broadcasted_iota(jnp.int32, (8, 128), 1)
    zeros = jnp.zeros((8, 128), jnp.int32)
    heads = [zeros + map_ref[pl.ds((ka * 32 + vert) * 4 + r, 1), :][:, 0:1] // 128 for r in range(4)]
    owned = [[(heads[r] >= o * 128) & (heads[r] < (o + 1) * 128) for r in range(3)] for o in range(4)]

    def pack(j, _):
        x2, w2 = (j // 4) % 2, (j // 8) * 4 + j % 4
        for u in range(3):
            unit = up_ref[j] if u == 0 else low_ref[2 * j + u - 1]
            runs = [unit[:, r * 128:(r + 1) * 128].astype(F32) for r in range(4)]
            for o in range(4):
                value = runs[3]
                for r in range(3):
                    value = jnp.where(owned[o][r], runs[r], value)
                if u == 0:
                    up_send[w2 * 8 + o * 2 + x2] = value.astype(BF16)
                else:
                    low_send[w2, o * 2 + x2, u - 1] = value.astype(BF16)
        return 0

    lax.fori_loop(0, 32, pack, 0)

    def clear(y, _):
        for n in range(3):
            acc[n, y] = jnp.zeros((2, 4, 64, 256), F32)
        return 0

    lax.fori_loop(0, 4, clear, 0)
    pl.semaphore_wait(barrier, 22)

    def give_up(w, p):
        send(up_send.at[w * 8 + p], up_recv.at[plane * 8 + row], s1.at[0], r1.at[0], (p // 2, (w // 4) * 8 + (p % 2) * 4 + w % 4))

    each(8, lambda k: say(ready, in_row((row + k) % 8)))

    def give_plane(k, _):
        give_up((plane + k) % 16, row)
        return 0

    def give_row(k, _):
        give_up(plane, (row + k) % 8)
        return 0

    lax.fori_loop(1, 16, give_plane, 0)
    lax.fori_loop(1, 8, give_row, 0)
    pl.semaphore_wait(ready, 7)

    def give_rest(k, _):
        give_up((plane + 1 + k // 7) % 16, (row + 1 + k % 7) % 8)
        return 0

    lax.fori_loop(0, 105, give_rest, 0)
    up_recv[plane * 8 + row] = up_send[plane * 8 + row]

    def find(g, found):
        block = map_ref[pl.ds(pl.multiple_of(g * 64, 64), 64), :][:, 0:1] // 128
        run = lax.broadcasted_iota(jnp.int32, (64, 512), 0) + g * 64
        device = run // 4
        place = ((device // 8) % 4 * 4 + device % 4) * 8 + device // 32 * 2 + device // 4 % 2
        hit = block == lax.broadcasted_iota(jnp.int32, (64, 512), 1)
        return jnp.maximum(found, jnp.max(jnp.where(hit, place, 0), axis=0, keepdims=True))

    table[...] = lax.fori_loop(0, 8, find, jnp.zeros((1, 512), jnp.int32))
    to_scalars = pltpu.make_async_copy(table, src_ref, in_sem.at[3])
    to_scalars.start()
    to_scalars.wait()
    take(up_recv.at[pl.ds(0, 127)], r1.at[0])

    def give_mid(k):
        w = (plane + k) % 16
        send(low_send.at[w], low_mid.at[plane], s1.at[1], r1.at[1], in_plane(w))

    each(16, give_mid)
    low_mid[plane] = low_send[plane]

    lives = [live_ref[2 * ka + b] for b in range(2)]

    def arrange_up(q, _):
        for n in range(16):
            block = q * 16 + n
            halves = []
            for b in range(2):
                s = src_ref[0, ka * 128 + b * 64 + block]
                tile = up_recv[s].astype(F32)
                halves.append(jnp.where(lane + block * 128 < lives[b], tile, 0.0))
            both = jnp.concatenate(halves, axis=0).astype(BF16)
            for c in range(CHAINS):
                if STARTS[c] <= n * 128 < STARTS[c] + WIDTHS[c]:
                    at = n * 128 - STARTS[c]
                    stages[c][q, :, at:at + 128] = both
        return 0

    lax.fori_loop(0, 4, arrange_up, 0)

    order = (4, 5, 2, 3, 0, 1)

    def pieces(c):
        return 7 if ORDERS[c][0] == "x" else 3

    for c in order:
        for k in range(1, 8):
            p = (row + k) % 8
            if ORDERS[c][0] != "x":
                if k % 2:
                    continue
            send(stages[c].at[p // 2], uppers[c].at[yy, xx, zz, ka], q_send.at[c], q_recv.at[c], in_row(p))
        uppers[c][yy, xx, zz, ka] = stages[c][ka]

    def arrange_low(v, _):
        for b in range(2):
            for h in range(2):
                block = 2 * v + h
                s = src_ref[0, ka * 128 + b * 64 + block]
                keep = lane + block * 128 < lives[b]
                both = jnp.concatenate(
                    [jnp.where(keep, low_recv[s // 8, s % 8, u].astype(F32), 0.0) for u in range(2)], axis=0
                ).astype(BF16)
                at = b * 256 + h * 128
                stage_low[(v // 8) * 4 + v % 4, (v // 4) % 2, :, at:at + 128] = both
        return 0

    def vid(y, x, z):
        return y * 8 + x * 4 + z

    sent = []

    where = {"y": yy, "x": xx, "z": zz}
    sizes = {"y": 4, "x": 2, "z": 4}

    def chain(c):
        u = uppers[c]
        first, second, last = ORDERS[c]
        done = []
        count = 0

        def region(fixed, have):
            idx = []
            for name in "yxz":
                if name in fixed:
                    idx.append(fixed[name])
                elif name in have:
                    idx.append(pl.ds(0, sizes[name]))
                else:
                    idx.append(where[name])
            return u.at[tuple(idx)]

        def go(ref, axis, step):
            nonlocal count
            to = dict(where)
            to[axis] = (where[axis] + step) % sizes[axis]
            copy = send(
                ref, ref, g_send.at[c, count], g_recv.at[c, count], (ka, vid(to["y"], to["x"], to["z"]))
            )
            count += 1
            sent.append(copy)
            return copy

        def both(axis, fixed, have):
            ref = region(fixed, have)
            if axis == "x":
                return [go(ref, axis, 1)]
            return [go(ref, axis, 1), go(ref, axis, 3)]

        def onward(pair, axis, fixed, have, cut):
            before, after = (where[axis] + 3) % 4, (where[axis] + 1) % 4
            halves = ({}, {})
            if cut == "x":
                halves = ({"x": 0}, {"x": 1})
            elif cut in ("y", "z"):
                halves = ({cut: pl.ds(0, 2)}, {cut: pl.ds(2, 2)})
            out = []
            for side, (copy, came, step) in enumerate(((pair[0], before, 1), (pair[1], after, 3))):
                copy.wait_recv()
                ref = region({**fixed, axis: came, **halves[side]}, have)
                if cut == "o":
                    ref = ref.at[pl.ds(2 * side, 2)]
                out.append(go(ref, axis, step))
            return out

        if first != "x":
            begun = both(first, {}, "")
            yield
            on = onward(begun, first, {}, "", "o")
            yield
            for copy in on:
                copy.wait_recv()
        cut = first
        here = where[second]
        middle = both(second, {}, first)
        if last == "x":
            batches = both(last, {second: here}, first)
        yield
        on = onward(middle, second, {}, first, cut)
        if last == "x":
            for step in (3, 1):
                batches += both(last, {second: (here + step) % 4}, first)
        yield
        for copy in on:
            copy.wait_recv()
        if last == "x":
            batches += both(last, {second: (here + 2) % 4}, first)
            yield
            for copy in batches:
                copy.wait_recv()
            yield
            return
        ends = both(last, {}, first + second)
        yield
        ends = onward(ends, last, {}, first + second, second)
        yield
        for copy in ends:
            copy.wait_recv()
        yield

    chains = [chain(c) for c in range(CHAINS)]

    def run(*names):
        for c in names:
            next(chains[c])

    core, side = ka % 2, ka // 2
    sibling = side * 2 + 1 - core

    def low_out(slot, h, x):
        return send(
            low_plane.at[:, x], low_all.at[core, side, xx], m_send.at[slot], m_recv.at[slot],
            (h * 2 + core, yy * 8 + x * 4 + zz),
        )

    moves = []
    def term(c, n, rows):
        flat = rows.reshape(-1, WIDTHS[c])
        value = lax.dot_general(
            flat, dip[n, :, STARTS[c]:STARTS[c] + WIDTHS[c]], NT, preferred_element_type=F32
        )
        return value

    def add_z(z):
        def body(n, _):
            acc[n, :, :, z] += (term(0, n, ua[:, :, z]) + term(4, n, ue[:, :, z])).reshape(4, 2, 64, 256)
            return 0

        lax.fori_loop(0, 3, body, 0)

    def add_y(y):
        def body(n, _):
            acc[n, y] += (term(1, n, ub[y]) + term(5, n, uf[y])).reshape(2, 4, 64, 256)
            return 0

        lax.fori_loop(0, 3, body, 0)

    def add_x(x):
        def body(n, _):
            acc[n, :, x] += (term(2, n, uc[:, x]) + term(3, n, ud[:, x])).reshape(4, 4, 64, 256)
            return 0

        lax.fori_loop(0, 3, body, 0)

    for c in order:
        take(stages[c].at[pl.ds(0, pieces(c))], q_recv.at[c])
        run(c)
    run(2, 3)
    run(4, 5)
    run(2, 3)
    run(0, 1)
    run(4, 5)
    take(low_mid.at[pl.ds(0, 15)], r1.at[1])

    def give_low(k):
        p = (row + k) % 8
        send(low_mid.at[:, p], low_recv.at[:, row], s2.at[1], r2.at[1], in_row(p))

    each(8, give_low)
    low_recv[:, row] = low_mid[:, row]
    run(2, 3)
    run(0, 1)
    run(2, 3)
    take(low_recv.at[:, pl.ds(0, 7)], r2.at[1])
    lax.fori_loop(0, 32, arrange_low, 0)

    def give_rows(k):
        w = (plane + k) % 16
        send(stage_low.at[w], low_plane.at[plane], l_send, l_recv, in_plane(w))

    each(16, give_rows)
    low_plane[plane] = stage_low[plane]
    for c in dips:
        c.wait()
    add_z(zz)
    add_y(yy)
    run(4, 5)
    take(low_plane.at[pl.ds(0, 15)], l_recv)
    moves.append(low_out(0, side, 1 - xx))
    moves.append(low_out(1, 1 - side, 1 - xx))
    moves.append(low_out(2, 1 - side, xx))
    low_all[core, side, xx] = low_plane[:, xx]
    add_x(xx)
    run(0, 1)

    def sides(k, _):
        add_z((zz + 3 - 2 * k) % 4)
        add_y((yy + 3 - 2 * k) % 4)
        return 0

    lax.fori_loop(0, 2, sides, 0)
    run(2, 3)
    add_x(1 - xx)
    for m in moves:
        m.wait_recv()
    moves.append(send(
        low_all.at[core], low_all.at[core], m_send.at[3], m_recv.at[3], (sibling, vert)
    ))
    run(4, 0)
    add_z((zz + 2) % 4)
    run(5, 1)
    add_y((yy + 2) % 4)
    moves[3].wait_recv()

    def factor(k, d):
        return rot_ref[d, k] * coup_ref[d, k].astype(F32)

    def step(g, _):
        y, x = g // 2, g % 2
        sums = [acc[n, y, x].reshape(4, 8, 8, 256) for n in range(3)]
        zero, up, down = sums
        rows = pl.ds(pl.multiple_of(g * 32, 32), 32)
        for k in range(8):
            value = factor(k, 0) * zero[:, k]
            if k < 7:
                value = value + factor(k, 1) * up[:, k + 1]
            if k > 0:
                value = value + factor(k, 2) * down[:, k - 1]
            half[rows, k * 256:(k + 1) * 256] = value.reshape(32, 256).astype(BF16)
        return 0

    lax.fori_loop(0, 8, step, 0)

    def amplitude(c, h):
        quarter = (h * 2 + c) * 4
        total = None
        for o in range(4):
            lows = low_all[o % 2, o // 2, :, pl.ds(quarter, 4)].reshape(128, 512)
            value = lax.dot_general(half[:, o * 512:(o + 1) * 512], lows, NT, preferred_element_type=F32)
            total = value if total is None else total + value
        amp[c, h] = total.reshape(32, 8, 128)

    def others(h, _):
        amplitude(1 - core, h)
        return 0

    def own(h, _):
        amplitude(core, h)
        return 0

    lax.fori_loop(0, 2, others, 0)
    to_pair = send(amp.at[1 - core], pair, s1.at[2], r1.at[2], (sibling, vert))
    lax.fori_loop(0, 2, own, 0)

    to_pair.wait_recv()
    pair[...] = pair[...] + amp[core]
    mine = side * 32 + vert

    def give(k, _):
        h2, v2 = (side + k // 32) % 2, (vert + k % 32) % 32
        send(pair.at[h2, v2], part.at[mine], s2.at[2], r2.at[2], (h2 * 2 + core, v2))
        return 0

    lax.fori_loop(1, 64, give, 0)
    part[mine] = pair[side, vert]
    take(up_send.at[pl.ds(0, 127)], s1.at[0])
    take(low_send.at[pl.ds(0, 15)], s1.at[1])
    take(low_recv.at[:, pl.ds(0, 7)], s2.at[1])
    for c in order:
        take(stages[c].at[pl.ds(0, pieces(c))], q_send.at[c])
    take(stage_low.at[pl.ds(0, 15)], l_send)
    for copy in sent + moves:
        copy.wait_send()
    to_pair.wait_send()
    take(part.at[pl.ds(0, 63)], s2.at[2])
    take(part.at[pl.ds(0, 63)], r2.at[2])
    total = jnp.sum(part[...], axis=0)
    out_ref[...] = total * total


def per_device(
    eig_lower, eig_upper, layout_map, block_live, coupling, rot_coef, dip_zero, dip_raise, dip_lower
):
    smem = pl.BlockSpec(memory_space=pltpu.SMEM)
    vmem = pl.BlockSpec(memory_space=pltpu.VMEM)
    hbm = pl.BlockSpec(memory_space=pl.ANY)
    dma = pltpu.SemaphoreType.DMA
    out = pl.pallas_call(
        kernel,
        out_shape=jax.ShapeDtypeStruct((8, 128), F32),
        in_specs=[smem] * 3 + [hbm] * 6,
        out_specs=vmem,
        scratch_shapes=[
            pltpu.VMEM((512, 128), jnp.int32),
            pltpu.VMEM((1, 512), jnp.int32),
            pltpu.SMEM((1, 512), jnp.int32),
            pltpu.VMEM((64, 8, 512), BF16),
            pltpu.VMEM((32, 8, 512), BF16),
            pltpu.VMEM((128, 8, 128), BF16),
            pltpu.VMEM((128, 8, 128), BF16),
            pltpu.VMEM((16, 8, 2, 8, 128), BF16),
            pltpu.VMEM((16, 8, 2, 8, 128), BF16),
            pltpu.VMEM((16, 8, 2, 8, 128), BF16),
            *[pltpu.VMEM((8, 16, w), BF16) for w in WIDTHS],
            *[pltpu.VMEM((4, 2, 4, 4, 16, w), BF16) for w in WIDTHS],
            pltpu.VMEM((16, 2, 16, 512), BF16),
            pltpu.VMEM((16, 2, 16, 512), BF16),
            pltpu.VMEM((2, 2, 2, 16, 16, 512), BF16),
            pltpu.VMEM((3, 256, 2048), BF16),
            pltpu.VMEM((3, 4, 2, 4, 64, 256), F32),
            pltpu.VMEM((256, 2048), BF16),
            pltpu.VMEM((2, 2, 32, 8, 128), F32),
            pltpu.VMEM((2, 32, 8, 128), F32),
            pltpu.VMEM((64, 8, 128), F32),
            pltpu.SemaphoreType.REGULAR,
            dma((4,)), dma((3,)),
            dma((3,)), dma((3,)), dma((3,)), dma((3,)),
            dma((CHAINS,)), dma((CHAINS,)),
            dma((CHAINS, 12)), dma((CHAINS, 12)),
            dma, dma,
            dma((4,)), dma((4,)),
        ],
        compiler_params=pltpu.CompilerParams(
            collective_id=0, has_side_effects=True, vmem_limit_bytes=60 * 1024 * 1024
        ),
        cost_estimate=pl.CostEstimate(flops=7_000_000_000, bytes_accessed=5_000_000, transcendentals=0),
    )(
        block_live, coupling.T, rot_coef.T, layout_map.reshape(512, 128),
        eig_lower.reshape(64, 8, 512), eig_upper.reshape(32, 8, 512), dip_zero, dip_raise, dip_lower,
    )
    return out.T


def solution(mesh):
    return jax.shard_map(
        per_device,
        mesh=mesh,
        in_specs=(
            P(None, ("ka", "vert")),
            P(None, ("ka", "vert")),
            P(),
            P(),
            P(),
            P(),
            P("vert", "ka"),
            P("vert", "ka"),
            P("vert", "ka"),
        ),
        out_specs=P("ka", "vert"),
        check_vma=False,
    )
```

```python
import jax
import jax.numpy as jnp
from jax import lax
from jax.experimental import pallas as pl
from jax.experimental.pallas import tpu as pltpu
from jax.sharding import PartitionSpec as P

F32 = jnp.float32
BF16 = jnp.bfloat16
MESH = pl.DeviceIdType.MESH
WIDTHS = (512, 512, 256, 256, 256, 256)
STARTS = (0, 512, 1024, 1280, 1536, 1792)
ORDERS = ("xyz", "xzy", "yzx", "zyx", "xyz", "xzy")
CHAINS = len(WIDTHS)
NT = (((1,), (1,)), ((), ()))


def kernel(
    live_ref, coup_ref, rot_ref, map_hbm, low_hbm, up_hbm, dz_hbm, dr_hbm, dl_hbm,
    out_ref,
    map_ref, table, src_ref, low_ref, up_ref, up_send, up_recv, low_send, low_mid, low_recv,
    sta, stb, stc, std_, ste, stf, ua, ub, uc, ud, ue, uf, stage_low, low_plane, low_all, dip, acc, half, amp, pair, part,
    ready, in_sem, dip_sem, s1, r1, s2, r2, q_send, q_recv, g_send, g_recv, l_send, l_recv, m_send, m_recv,
):
    ka = lax.axis_index("ka")
    vert = lax.axis_index("vert")
    yy = vert // 8
    xx = (vert // 4) % 2
    zz = vert % 4
    row = ka * 2 + xx
    plane = yy * 4 + zz
    stages = (sta, stb, stc, std_, ste, stf)
    uppers = (ua, ub, uc, ud, ue, uf)

    def in_row(p):
        return p // 2, yy * 8 + (p % 2) * 4 + zz

    def in_plane(w):
        return ka, (w // 4) * 8 + xx * 4 + w % 4

    def say(sem, to):
        pl.semaphore_signal(sem, inc=1, device_id=to, device_id_type=MESH)

    def take(ref, sem):
        pltpu.make_async_copy(ref, ref, sem).wait()

    def send(src, dst, out_sem, in_sem_, to):
        copy = pltpu.make_async_remote_copy(
            src_ref=src, dst_ref=dst, send_sem=out_sem, recv_sem=in_sem_, device_id=to, device_id_type=MESH
        )
        copy.start()
        return copy

    barrier = pltpu.get_barrier_semaphore()
    def each(count, body):
        def step(k, _):
            body(k)
            return 0

        lax.fori_loop(1, count, step, 0)

    each(8, lambda k: say(barrier, in_row((row + k) % 8)))
    each(16, lambda k: say(barrier, in_plane((plane + k) % 16)))
    loads = [pltpu.make_async_copy(h, v, in_sem.at[n]) for n, (h, v) in enumerate(((map_hbm, map_ref), (up_hbm, up_ref), (low_hbm, low_ref)))]
    dips = [pltpu.make_async_copy(h, dip.at[n], dip_sem.at[n]) for n, h in enumerate((dz_hbm, dr_hbm, dl_hbm))]
    for c in loads + dips:
        c.start()
    for c in loads:
        c.wait()

    lane = lax.broadcasted_iota(jnp.int32, (8, 128), 1)
    zeros = jnp.zeros((8, 128), jnp.int32)
    heads = [zeros + map_ref[pl.ds((ka * 32 + vert) * 4 + r, 1), :][:, 0:1] // 128 for r in range(4)]
    owned = [[(heads[r] >= o * 128) & (heads[r] < (o + 1) * 128) for r in range(3)] for o in range(4)]

    def pack(j, _):
        x2, w2 = (j // 4) % 2, (j // 8) * 4 + j % 4
        for u in range(3):
            unit = up_ref[j] if u == 0 else low_ref[2 * j + u - 1]
            runs = [unit[:, r * 128:(r + 1) * 128].astype(F32) for r in range(4)]
            for o in range(4):
                value = runs[3]
                for r in range(3):
                    value = jnp.where(owned[o][r], runs[r], value)
                if u == 0:
                    up_send[w2 * 8 + o * 2 + x2] = value.astype(BF16)
                else:
                    low_send[w2, o * 2 + x2, u - 1] = value.astype(BF16)
        return 0

    lax.fori_loop(0, 32, pack, 0)

    def clear(y, _):
        for n in range(3):
            acc[n, y] = jnp.zeros((2, 4, 64, 256), F32)
        return 0

    lax.fori_loop(0, 4, clear, 0)
    pl.semaphore_wait(barrier, 22)

    def give_up(w, p):
        send(up_send.at[w * 8 + p], up_recv.at[plane * 8 + row], s1.at[0], r1.at[0], (p // 2, (w // 4) * 8 + (p % 2) * 4 + w % 4))

    each(8, lambda k: say(ready, in_row((row + k) % 8)))

    def give_plane(k, _):
        give_up((plane + k) % 16, row)
        return 0

    def give_row(k, _):
        give_up(plane, (row + k) % 8)
        return 0

    lax.fori_loop(1, 16, give_plane, 0)
    lax.fori_loop(1, 8, give_row, 0)
    pl.semaphore_wait(ready, 7)

    def give_rest(k, _):
        give_up((plane + 1 + k // 7) % 16, (row + 1 + k % 7) % 8)
        return 0

    lax.fori_loop(0, 105, give_rest, 0)

    def give_mid(k):
        w = (plane + k) % 16
        send(low_send.at[w], low_mid.at[plane], s1.at[1], r1.at[1], in_plane(w))

    each(16, give_mid)
    low_mid[plane] = low_send[plane]
    up_recv[plane * 8 + row] = up_send[plane * 8 + row]

    def find(g, found):
        block = map_ref[pl.ds(pl.multiple_of(g * 64, 64), 64), :][:, 0:1] // 128
        run = lax.broadcasted_iota(jnp.int32, (64, 512), 0) + g * 64
        device = run // 4
        place = ((device // 8) % 4 * 4 + device % 4) * 8 + device // 32 * 2 + device // 4 % 2
        hit = block == lax.broadcasted_iota(jnp.int32, (64, 512), 1)
        return jnp.maximum(found, jnp.max(jnp.where(hit, place, 0), axis=0, keepdims=True))

    table[...] = lax.fori_loop(0, 8, find, jnp.zeros((1, 512), jnp.int32))
    to_scalars = pltpu.make_async_copy(table, src_ref, in_sem.at[3])
    to_scalars.start()
    to_scalars.wait()
    take(up_recv.at[pl.ds(0, 127)], r1.at[0])

    lives = [live_ref[2 * ka + b] for b in range(2)]

    def arrange_up(q, _):
        for n in range(16):
            block = q * 16 + n
            halves = []
            for b in range(2):
                s = src_ref[0, ka * 128 + b * 64 + block]
                tile = up_recv[s].astype(F32)
                halves.append(jnp.where(lane + block * 128 < lives[b], tile, 0.0))
            both = jnp.concatenate(halves, axis=0).astype(BF16)
            for c in range(CHAINS):
                if STARTS[c] <= n * 128 < STARTS[c] + WIDTHS[c]:
                    at = n * 128 - STARTS[c]
                    stages[c][q, :, at:at + 128] = both
        return 0

    lax.fori_loop(0, 4, arrange_up, 0)

    order = (2, 3, 4, 5, 0, 1)

    def pieces(c):
        return 7 if ORDERS[c][0] == "x" else 3

    for c in order:
        for k in range(1, 8):
            p = (row + k) % 8
            if ORDERS[c][0] != "x":
                if k % 2:
                    continue
            send(stages[c].at[p // 2], uppers[c].at[yy, xx, zz, ka], q_send.at[c], q_recv.at[c], in_row(p))
        uppers[c][yy, xx, zz, ka] = stages[c][ka]

    def arrange_low(v, _):
        for b in range(2):
            for h in range(2):
                block = 2 * v + h
                s = src_ref[0, ka * 128 + b * 64 + block]
                keep = lane + block * 128 < lives[b]
                both = jnp.concatenate(
                    [jnp.where(keep, low_recv[s // 8, s % 8, u].astype(F32), 0.0) for u in range(2)], axis=0
                ).astype(BF16)
                at = b * 256 + h * 128
                stage_low[(v // 8) * 4 + v % 4, (v // 4) % 2, :, at:at + 128] = both
        return 0

    def vid(y, x, z):
        return y * 8 + x * 4 + z

    sent = []

    where = {"y": yy, "x": xx, "z": zz}
    sizes = {"y": 4, "x": 2, "z": 4}

    def chain(c):
        u = uppers[c]
        first, second, last = ORDERS[c]
        done = []
        count = 0

        def region(fixed, have):
            idx = []
            for name in "yxz":
                if name in fixed:
                    idx.append(fixed[name])
                elif name in have:
                    idx.append(pl.ds(0, sizes[name]))
                else:
                    idx.append(where[name])
            return u.at[tuple(idx)]

        def go(ref, axis, step):
            nonlocal count
            to = dict(where)
            to[axis] = (where[axis] + step) % sizes[axis]
            copy = send(
                ref, ref, g_send.at[c, count], g_recv.at[c, count], (ka, vid(to["y"], to["x"], to["z"]))
            )
            count += 1
            sent.append(copy)
            return copy

        def both(axis, fixed, have):
            ref = region(fixed, have)
            if axis == "x":
                return [go(ref, axis, 1)]
            return [go(ref, axis, 1), go(ref, axis, 3)]

        def onward(pair, axis, fixed, have, cut):
            before, after = (where[axis] + 3) % 4, (where[axis] + 1) % 4
            halves = ({}, {})
            if cut == "x":
                halves = ({"x": 0}, {"x": 1})
            elif cut in ("y", "z"):
                halves = ({cut: pl.ds(0, 2)}, {cut: pl.ds(2, 2)})
            out = []
            for side, (copy, came, step) in enumerate(((pair[0], before, 1), (pair[1], after, 3))):
                copy.wait_recv()
                ref = region({**fixed, axis: came, **halves[side]}, have)
                if cut == "o":
                    ref = ref.at[pl.ds(2 * side, 2)]
                out.append(go(ref, axis, step))
            return out

        if first != "x":
            begun = both(first, {}, "")
            yield
            on = onward(begun, first, {}, "", "o")
            yield
            for copy in on:
                copy.wait_recv()
        cut = first
        here = where[second]
        middle = both(second, {}, first)
        if last == "x":
            batches = both(last, {second: here}, first)
        yield
        on = onward(middle, second, {}, first, cut)
        if last == "x":
            for step in (3, 1):
                batches += both(last, {second: (here + step) % 4}, first)
        yield
        for copy in on:
            copy.wait_recv()
        if last == "x":
            batches += both(last, {second: (here + 2) % 4}, first)
            yield
            for copy in batches:
                copy.wait_recv()
            yield
            return
        ends = both(last, {}, first + second)
        yield
        ends = onward(ends, last, {}, first + second, second)
        yield
        for copy in ends:
            copy.wait_recv()
        yield

    chains = [chain(c) for c in range(CHAINS)]

    def run(*names):
        for c in names:
            next(chains[c])

    core, side = ka % 2, ka // 2
    sibling = side * 2 + 1 - core

    def low_out(slot, h, x):
        return send(
            low_plane.at[:, x], low_all.at[core, side, xx], m_send.at[slot], m_recv.at[slot],
            (h * 2 + core, yy * 8 + x * 4 + zz),
        )

    moves = []
    def term(c, n, rows):
        flat = rows.reshape(-1, WIDTHS[c])
        value = lax.dot_general(
            flat, dip[n, :, STARTS[c]:STARTS[c] + WIDTHS[c]], NT, preferred_element_type=F32
        )
        return value

    def add_z(z):
        def body(n, _):
            acc[n, :, :, z] += (term(0, n, ua[:, :, z]) + term(4, n, ue[:, :, z])).reshape(4, 2, 64, 256)
            return 0

        lax.fori_loop(0, 3, body, 0)

    def add_y(y):
        def body(n, _):
            acc[n, y] += (term(1, n, ub[y]) + term(5, n, uf[y])).reshape(2, 4, 64, 256)
            return 0

        lax.fori_loop(0, 3, body, 0)

    def add_x(x):
        def body(n, _):
            acc[n, :, x] += (term(2, n, uc[:, x]) + term(3, n, ud[:, x])).reshape(4, 4, 64, 256)
            return 0

        lax.fori_loop(0, 3, body, 0)

    take(low_mid.at[pl.ds(0, 15)], r1.at[1])

    def give_low(k):
        p = (row + k) % 8
        send(low_mid.at[:, p], low_recv.at[:, row], s2.at[1], r2.at[1], in_row(p))

    each(8, give_low)
    low_recv[:, row] = low_mid[:, row]
    for c in order:
        take(stages[c].at[pl.ds(0, pieces(c))], q_recv.at[c])
        run(c)
    run(2, 3)
    run(4, 5)
    run(2, 3)
    run(0, 1)
    take(low_recv.at[:, pl.ds(0, 7)], r2.at[1])
    lax.fori_loop(0, 32, arrange_low, 0)

    def give_rows(k):
        w = (plane + k) % 16
        send(stage_low.at[w], low_plane.at[plane], l_send, l_recv, in_plane(w))

    each(16, give_rows)
    low_plane[plane] = stage_low[plane]
    run(4, 5)
    run(2, 3)
    run(0, 1)
    run(2, 3)
    for c in dips:
        c.wait()
    add_z(zz)
    add_y(yy)
    run(4, 5)
    take(low_plane.at[pl.ds(0, 15)], l_recv)
    moves.append(low_out(0, side, 1 - xx))
    moves.append(low_out(1, 1 - side, 1 - xx))
    moves.append(low_out(2, 1 - side, xx))
    low_all[core, side, xx] = low_plane[:, xx]
    add_x(xx)
    run(0, 1)

    def sides(k, _):
        add_z((zz + 3 - 2 * k) % 4)
        add_y((yy + 3 - 2 * k) % 4)
        return 0

    lax.fori_loop(0, 2, sides, 0)
    run(2, 3)
    add_x(1 - xx)
    for m in moves:
        m.wait_recv()
    moves.append(send(
        low_all.at[core], low_all.at[core], m_send.at[3], m_recv.at[3], (sibling, vert)
    ))
    run(4, 0)
    add_z((zz + 2) % 4)
    run(5, 1)
    add_y((yy + 2) % 4)
    moves[3].wait_recv()

    def factor(k, d):
        return rot_ref[d, k] * coup_ref[d, k].astype(F32)

    def step(g, _):
        y, x = g // 2, g % 2
        sums = [acc[n, y, x].reshape(4, 8, 8, 256) for n in range(3)]
        zero, up, down = sums
        rows = pl.ds(pl.multiple_of(g * 32, 32), 32)
        for k in range(8):
            value = factor(k, 0) * zero[:, k]
            if k < 7:
                value = value + factor(k, 1) * up[:, k + 1]
            if k > 0:
                value = value + factor(k, 2) * down[:, k - 1]
            half[rows, k * 256:(k + 1) * 256] = value.reshape(32, 256).astype(BF16)
        return 0

    lax.fori_loop(0, 8, step, 0)

    def amplitude(c, h):
        quarter = (h * 2 + c) * 4
        total = None
        for o in range(4):
            lows = low_all[o % 2, o // 2, :, pl.ds(quarter, 4)].reshape(128, 512)
            value = lax.dot_general(half[:, o * 512:(o + 1) * 512], lows, NT, preferred_element_type=F32)
            total = value if total is None else total + value
        amp[c, h] = total.reshape(32, 8, 128)

    def others(h, _):
        amplitude(1 - core, h)
        return 0

    def own(h, _):
        amplitude(core, h)
        return 0

    lax.fori_loop(0, 2, others, 0)
    to_pair = send(amp.at[1 - core], pair, s1.at[2], r1.at[2], (sibling, vert))
    lax.fori_loop(0, 2, own, 0)

    to_pair.wait_recv()
    pair[...] = pair[...] + amp[core]
    mine = side * 32 + vert

    def give(k, _):
        h2, v2 = (side + k // 32) % 2, (vert + k % 32) % 32
        send(pair.at[h2, v2], part.at[mine], s2.at[2], r2.at[2], (h2 * 2 + core, v2))
        return 0

    lax.fori_loop(1, 64, give, 0)
    part[mine] = pair[side, vert]
    take(up_send.at[pl.ds(0, 127)], s1.at[0])
    take(low_send.at[pl.ds(0, 15)], s1.at[1])
    take(low_recv.at[:, pl.ds(0, 7)], s2.at[1])
    for c in order:
        take(stages[c].at[pl.ds(0, pieces(c))], q_send.at[c])
    take(stage_low.at[pl.ds(0, 15)], l_send)
    for copy in sent + moves:
        copy.wait_send()
    to_pair.wait_send()
    take(part.at[pl.ds(0, 63)], s2.at[2])
    take(part.at[pl.ds(0, 63)], r2.at[2])
    total = jnp.sum(part[...], axis=0)
    out_ref[...] = total * total


def per_device(
    eig_lower, eig_upper, layout_map, block_live, coupling, rot_coef, dip_zero, dip_raise, dip_lower
):
    smem = pl.BlockSpec(memory_space=pltpu.SMEM)
    vmem = pl.BlockSpec(memory_space=pltpu.VMEM)
    hbm = pl.BlockSpec(memory_space=pl.ANY)
    dma = pltpu.SemaphoreType.DMA
    out = pl.pallas_call(
        kernel,
        out_shape=jax.ShapeDtypeStruct((8, 128), F32),
        in_specs=[smem] * 3 + [hbm] * 6,
        out_specs=vmem,
        scratch_shapes=[
            pltpu.VMEM((512, 128), jnp.int32),
            pltpu.VMEM((1, 512), jnp.int32),
            pltpu.SMEM((1, 512), jnp.int32),
            pltpu.VMEM((64, 8, 512), BF16),
            pltpu.VMEM((32, 8, 512), BF16),
            pltpu.VMEM((128, 8, 128), BF16),
            pltpu.VMEM((128, 8, 128), BF16),
            pltpu.VMEM((16, 8, 2, 8, 128), BF16),
            pltpu.VMEM((16, 8, 2, 8, 128), BF16),
            pltpu.VMEM((16, 8, 2, 8, 128), BF16),
            *[pltpu.VMEM((8, 16, w), BF16) for w in WIDTHS],
            *[pltpu.VMEM((4, 2, 4, 4, 16, w), BF16) for w in WIDTHS],
            pltpu.VMEM((16, 2, 16, 512), BF16),
            pltpu.VMEM((16, 2, 16, 512), BF16),
            pltpu.VMEM((2, 2, 2, 16, 16, 512), BF16),
            pltpu.VMEM((3, 256, 2048), BF16),
            pltpu.VMEM((3, 4, 2, 4, 64, 256), F32),
            pltpu.VMEM((256, 2048), BF16),
            pltpu.VMEM((2, 2, 32, 8, 128), F32),
            pltpu.VMEM((2, 32, 8, 128), F32),
            pltpu.VMEM((64, 8, 128), F32),
            pltpu.SemaphoreType.REGULAR,
            dma((4,)), dma((3,)),
            dma((3,)), dma((3,)), dma((3,)), dma((3,)),
            dma((CHAINS,)), dma((CHAINS,)),
            dma((CHAINS, 12)), dma((CHAINS, 12)),
            dma, dma,
            dma((4,)), dma((4,)),
        ],
        compiler_params=pltpu.CompilerParams(
            collective_id=0, has_side_effects=True, vmem_limit_bytes=60 * 1024 * 1024
        ),
        cost_estimate=pl.CostEstimate(flops=7_000_000_000, bytes_accessed=5_000_000, transcendentals=0),
    )(
        block_live, coupling.T, rot_coef.T, layout_map.reshape(512, 128),
        eig_lower.reshape(64, 8, 512), eig_upper.reshape(32, 8, 512), dip_zero, dip_raise, dip_lower,
    )
    return out.T


def solution(mesh):
    return jax.shard_map(
        per_device,
        mesh=mesh,
        in_specs=(
            P(None, ("ka", "vert")),
            P(None, ("ka", "vert")),
            P(),
            P(),
            P(),
            P(),
            P("vert", "ka"),
            P("vert", "ka"),
            P("vert", "ka"),
        ),
        out_specs=P("ka", "vert"),
        check_vma=False,
    )
```

```python
import jax
import jax.numpy as jnp
from jax import lax
from jax.experimental import pallas as pl
from jax.experimental.pallas import tpu as pltpu
from jax.sharding import PartitionSpec as P

F32 = jnp.float32
BF16 = jnp.bfloat16
MESH = pl.DeviceIdType.MESH
WIDTHS = (512, 512, 256, 256, 256, 256)
STARTS = (0, 512, 1024, 1280, 1536, 1792)
ORDERS = ("xyz", "xzy", "yzx", "zyx", "xyz", "xzy")
CHAINS = len(WIDTHS)
NT = (((1,), (1,)), ((), ()))


def kernel(
    live_ref, coup_ref, rot_ref, map_hbm, low_hbm, up_hbm, dz_hbm, dr_hbm, dl_hbm,
    out_ref,
    map_ref, table, src_ref, low_ref, up_ref, up_send, up_recv, low_send, low_mid, low_recv,
    sta, stb, stc, std_, ste, stf, ua, ub, uc, ud, ue, uf, stage_low, low_plane, low_all, dip, acc, half, amp, pair, part,
    ready, in_sem, dip_sem, s1, r1, s2, r2, q_send, q_recv, g_send, g_recv, l_send, l_recv, m_send, m_recv,
):
    ka = lax.axis_index("ka")
    vert = lax.axis_index("vert")
    yy = vert // 8
    xx = (vert // 4) % 2
    zz = vert % 4
    row = ka * 2 + xx
    plane = yy * 4 + zz
    stages = (sta, stb, stc, std_, ste, stf)
    uppers = (ua, ub, uc, ud, ue, uf)

    def in_row(p):
        return p // 2, yy * 8 + (p % 2) * 4 + zz

    def in_plane(w):
        return ka, (w // 4) * 8 + xx * 4 + w % 4

    def say(sem, to):
        pl.semaphore_signal(sem, inc=1, device_id=to, device_id_type=MESH)

    def take(ref, sem):
        pltpu.make_async_copy(ref, ref, sem).wait()

    def send(src, dst, out_sem, in_sem_, to):
        copy = pltpu.make_async_remote_copy(
            src_ref=src, dst_ref=dst, send_sem=out_sem, recv_sem=in_sem_, device_id=to, device_id_type=MESH
        )
        copy.start()
        return copy

    barrier = pltpu.get_barrier_semaphore()
    def each(count, body):
        def step(k, _):
            body(k)
            return 0

        lax.fori_loop(1, count, step, 0)

    each(8, lambda k: say(barrier, in_row((row + k) % 8)))
    each(16, lambda k: say(barrier, in_plane((plane + k) % 16)))
    loads = [pltpu.make_async_copy(h, v, in_sem.at[n]) for n, (h, v) in enumerate(((map_hbm, map_ref), (up_hbm, up_ref), (low_hbm, low_ref)))]
    dips = [pltpu.make_async_copy(h, dip.at[n], dip_sem.at[n]) for n, h in enumerate((dz_hbm, dr_hbm, dl_hbm))]
    for c in loads + dips:
        c.start()
    for c in loads:
        c.wait()

    lane = lax.broadcasted_iota(jnp.int32, (8, 128), 1)
    zeros = jnp.zeros((8, 128), jnp.int32)
    heads = [zeros + map_ref[pl.ds((ka * 32 + vert) * 4 + r, 1), :][:, 0:1] // 128 for r in range(4)]
    owned = [[(heads[r] >= o * 128) & (heads[r] < (o + 1) * 128) for r in range(3)] for o in range(4)]

    def pack(j, _):
        x2, w2 = (j // 4) % 2, (j // 8) * 4 + j % 4
        for u in range(3):
            unit = up_ref[j] if u == 0 else low_ref[2 * j + u - 1]
            runs = [unit[:, r * 128:(r + 1) * 128].astype(F32) for r in range(4)]
            for o in range(4):
                value = runs[3]
                for r in range(3):
                    value = jnp.where(owned[o][r], runs[r], value)
                if u == 0:
                    up_send[w2 * 8 + o * 2 + x2] = value.astype(BF16)
                else:
                    low_send[w2, o * 2 + x2, u - 1] = value.astype(BF16)
        return 0

    lax.fori_loop(0, 32, pack, 0)

    def clear(y, _):
        for n in range(3):
            acc[n, y] = jnp.zeros((2, 4, 64, 256), F32)
        return 0

    lax.fori_loop(0, 4, clear, 0)
    pl.semaphore_wait(barrier, 22)

    def give_up(w, p):
        send(up_send.at[w * 8 + p], up_recv.at[plane * 8 + row], s1.at[0], r1.at[0], (p // 2, (w // 4) * 8 + (p % 2) * 4 + w % 4))

    each(8, lambda k: say(ready, in_row((row + k) % 8)))

    def give_plane(k, _):
        give_up((plane + k) % 16, row)
        return 0

    def give_row(k, _):
        give_up(plane, (row + k) % 8)
        return 0

    lax.fori_loop(1, 16, give_plane, 0)
    lax.fori_loop(1, 8, give_row, 0)
    pl.semaphore_wait(ready, 7)

    def give_rest(k, _):
        give_up((plane + 1 + k // 7) % 16, (row + 1 + k % 7) % 8)
        return 0

    lax.fori_loop(0, 105, give_rest, 0)

    def give_mid(k):
        w = (plane + k) % 16
        send(low_send.at[w], low_mid.at[plane], s1.at[1], r1.at[1], in_plane(w))

    each(16, give_mid)
    low_mid[plane] = low_send[plane]
    up_recv[plane * 8 + row] = up_send[plane * 8 + row]

    def find(g, found):
        block = map_ref[pl.ds(pl.multiple_of(g * 64, 64), 64), :][:, 0:1] // 128
        run = lax.broadcasted_iota(jnp.int32, (64, 512), 0) + g * 64
        device = run // 4
        place = ((device // 8) % 4 * 4 + device % 4) * 8 + device // 32 * 2 + device // 4 % 2
        hit = block == lax.broadcasted_iota(jnp.int32, (64, 512), 1)
        return jnp.maximum(found, jnp.max(jnp.where(hit, place, 0), axis=0, keepdims=True))

    table[...] = lax.fori_loop(0, 8, find, jnp.zeros((1, 512), jnp.int32))
    to_scalars = pltpu.make_async_copy(table, src_ref, in_sem.at[3])
    to_scalars.start()
    to_scalars.wait()
    take(up_recv.at[pl.ds(0, 127)], r1.at[0])

    lives = [live_ref[2 * ka + b] for b in range(2)]

    def arrange_up(q, _):
        for n in range(16):
            block = q * 16 + n
            halves = []
            for b in range(2):
                s = src_ref[0, ka * 128 + b * 64 + block]
                tile = up_recv[s].astype(F32)
                halves.append(jnp.where(lane + block * 128 < lives[b], tile, 0.0))
            both = jnp.concatenate(halves, axis=0).astype(BF16)
            for c in range(CHAINS):
                if STARTS[c] <= n * 128 < STARTS[c] + WIDTHS[c]:
                    at = n * 128 - STARTS[c]
                    stages[c][q, :, at:at + 128] = both
        return 0

    lax.fori_loop(0, 4, arrange_up, 0)

    order = (2, 3, 4, 5, 0, 1)

    def pieces(c):
        return 7 if ORDERS[c][0] == "x" else 3

    for c in order:
        for k in range(1, 8):
            p = (row + k) % 8
            if ORDERS[c][0] != "x":
                if k % 2:
                    continue
            send(stages[c].at[p // 2], uppers[c].at[yy, xx, zz, ka], q_send.at[c], q_recv.at[c], in_row(p))
        uppers[c][yy, xx, zz, ka] = stages[c][ka]

    def arrange_low(v, _):
        for b in range(2):
            for h in range(2):
                block = 2 * v + h
                s = src_ref[0, ka * 128 + b * 64 + block]
                keep = lane + block * 128 < lives[b]
                both = jnp.concatenate(
                    [jnp.where(keep, low_recv[s // 8, s % 8, u].astype(F32), 0.0) for u in range(2)], axis=0
                ).astype(BF16)
                at = b * 256 + h * 128
                stage_low[(v // 8) * 4 + v % 4, (v // 4) % 2, :, at:at + 128] = both
        return 0

    def vid(y, x, z):
        return y * 8 + x * 4 + z

    sent = []

    where = {"y": yy, "x": xx, "z": zz}
    sizes = {"y": 4, "x": 2, "z": 4}

    def chain(c):
        u = uppers[c]
        first, second, last = ORDERS[c]
        done = []
        count = 0

        def region(fixed, have):
            idx = []
            for name in "yxz":
                if name in fixed:
                    idx.append(fixed[name])
                elif name in have:
                    idx.append(pl.ds(0, sizes[name]))
                else:
                    idx.append(where[name])
            return u.at[tuple(idx)]

        def go(ref, axis, step):
            nonlocal count
            to = dict(where)
            to[axis] = (where[axis] + step) % sizes[axis]
            copy = send(
                ref, ref, g_send.at[c, count], g_recv.at[c, count], (ka, vid(to["y"], to["x"], to["z"]))
            )
            count += 1
            sent.append(copy)
            return copy

        def both(axis, fixed, have):
            ref = region(fixed, have)
            if axis == "x":
                return [go(ref, axis, 1)]
            return [go(ref, axis, 1), go(ref, axis, 3)]

        def onward(pair, axis, fixed, have, cut):
            before, after = (where[axis] + 3) % 4, (where[axis] + 1) % 4
            halves = ({}, {})
            if cut == "x":
                halves = ({"x": 0}, {"x": 1})
            elif cut in ("y", "z"):
                halves = ({cut: pl.ds(0, 2)}, {cut: pl.ds(2, 2)})
            out = []
            for side, (copy, came, step) in enumerate(((pair[0], before, 1), (pair[1], after, 3))):
                copy.wait_recv()
                ref = region({**fixed, axis: came, **halves[side]}, have)
                if cut == "o":
                    ref = ref.at[pl.ds(2 * side, 2)]
                out.append(go(ref, axis, step))
            return out

        if first != "x":
            begun = both(first, {}, "")
            yield
            on = onward(begun, first, {}, "", "o")
            yield
            for copy in on:
                copy.wait_recv()
        cut = first
        here = where[second]
        middle = both(second, {}, first)
        if last == "x":
            batches = both(last, {second: here}, first)
        yield
        on = onward(middle, second, {}, first, cut)
        if last == "x":
            for step in (3, 1):
                batches += both(last, {second: (here + step) % 4}, first)
        yield
        for copy in on:
            copy.wait_recv()
        if last == "x":
            batches += both(last, {second: (here + 2) % 4}, first)
            yield
            for copy in batches:
                copy.wait_recv()
            yield
            return
        ends = both(last, {}, first + second)
        yield
        ends = onward(ends, last, {}, first + second, second)
        yield
        for copy in ends:
            copy.wait_recv()
        yield

    chains = [chain(c) for c in range(CHAINS)]

    def run(*names):
        for c in names:
            next(chains[c])

    core, side = ka % 2, ka // 2
    sibling = side * 2 + 1 - core

    def low_out(slot, h, x):
        return send(
            low_plane.at[:, x], low_all.at[core, side, xx], m_send.at[slot], m_recv.at[slot],
            (h * 2 + core, yy * 8 + x * 4 + zz),
        )

    moves = []
    def term(c, n, rows):
        flat = rows.reshape(-1, WIDTHS[c])
        value = lax.dot_general(
            flat, dip[n, :, STARTS[c]:STARTS[c] + WIDTHS[c]], NT, preferred_element_type=F32
        )
        return value

    def add_z(z):
        def body(n, _):
            acc[n, :, :, z] += (term(0, n, ua[:, :, z]) + term(4, n, ue[:, :, z])).reshape(4, 2, 64, 256)
            return 0

        lax.fori_loop(0, 3, body, 0)

    def add_y(y):
        def body(n, _):
            acc[n, y] += (term(1, n, ub[y]) + term(5, n, uf[y])).reshape(2, 4, 64, 256)
            return 0

        lax.fori_loop(0, 3, body, 0)

    def add_x(x):
        def body(n, _):
            acc[n, :, x] += (term(2, n, uc[:, x]) + term(3, n, ud[:, x])).reshape(4, 4, 64, 256)
            return 0

        lax.fori_loop(0, 3, body, 0)

    take(low_mid.at[pl.ds(0, 15)], r1.at[1])

    def give_low(k):
        p = (row + k) % 8
        send(low_mid.at[:, p], low_recv.at[:, row], s2.at[1], r2.at[1], in_row(p))

    each(8, give_low)
    low_recv[:, row] = low_mid[:, row]
    for c in order:
        take(stages[c].at[pl.ds(0, pieces(c))], q_recv.at[c])
        run(c)
    run(2, 3)
    run(4, 5)
    run(2, 3)
    run(0, 1)
    take(low_recv.at[:, pl.ds(0, 7)], r2.at[1])
    lax.fori_loop(0, 32, arrange_low, 0)

    def give_rows(k):
        w = (plane + k) % 16
        send(stage_low.at[w], low_plane.at[plane], l_send, l_recv, in_plane(w))

    each(16, give_rows)
    low_plane[plane] = stage_low[plane]
    run(4, 5)
    run(2, 3)
    run(0, 1)
    run(2, 3)
    for c in dips:
        c.wait()
    add_z(zz)
    add_y(yy)
    run(4, 5)
    take(low_plane.at[pl.ds(0, 15)], l_recv)
    moves.append(low_out(0, side, 1 - xx))
    moves.append(low_out(1, 1 - side, 1 - xx))
    moves.append(low_out(2, 1 - side, xx))
    low_all[core, side, xx] = low_plane[:, xx]
    add_x(xx)
    run(0, 1)

    def sides(k, _):
        add_z((zz + 3 - 2 * k) % 4)
        add_y((yy + 3 - 2 * k) % 4)
        return 0

    lax.fori_loop(0, 2, sides, 0)
    run(2, 3)
    add_x(1 - xx)
    for m in moves:
        m.wait_recv()
    moves.append(send(
        low_all.at[core], low_all.at[core], m_send.at[3], m_recv.at[3], (sibling, vert)
    ))
    run(4, 0)
    add_z((zz + 2) % 4)
    run(5, 1)
    add_y((yy + 2) % 4)
    moves[3].wait_recv()

    def factor(k, d):
        return rot_ref[d, k] * coup_ref[d, k].astype(F32)

    def step(g, _):
        y, x = g // 2, g % 2
        sums = [acc[n, y, x].reshape(4, 8, 8, 256) for n in range(3)]
        zero, up, down = sums
        rows = pl.ds(pl.multiple_of(g * 32, 32), 32)
        for k in range(8):
            value = factor(k, 0) * zero[:, k]
            if k < 7:
                value = value + factor(k, 1) * up[:, k + 1]
            if k > 0:
                value = value + factor(k, 2) * down[:, k - 1]
            half[rows, k * 256:(k + 1) * 256] = value.reshape(32, 256).astype(BF16)
        return 0

    lax.fori_loop(0, 8, step, 0)

    def amplitude(c, h):
        quarter = (h * 2 + c) * 4
        total = None
        for o in range(4):
            lows = low_all[o % 2, o // 2, :, pl.ds(quarter, 4)].reshape(128, 512)
            value = lax.dot_general(half[:, o * 512:(o + 1) * 512], lows, NT, preferred_element_type=F32)
            total = value if total is None else total + value
        amp[c, h] = total.reshape(32, 8, 128)

    to_pair = []
    for n in range(2):
        h = (side + n) % 2
        amplitude(1 - core, h)
        to_pair.append(send(amp.at[1 - core, h], pair.at[h], s1.at[2 + n], r1.at[2 + n], (sibling, vert)))

    mine = side * 32 + vert
    for n in range(2):
        h = (side + n) % 2
        amplitude(core, h)
        to_pair[n].wait_recv()
        pair[h] = pair[h] + amp[core, h]

        def give(k, _):
            v2 = (vert + k) % 32
            send(pair.at[h, v2], part.at[mine], s2.at[2], r2.at[2], (h * 2 + core, v2))
            return 0

        lax.fori_loop(1 - n, 32, give, 0)
    part[mine] = pair[side, vert]
    take(up_send.at[pl.ds(0, 127)], s1.at[0])
    take(low_send.at[pl.ds(0, 15)], s1.at[1])
    take(low_recv.at[:, pl.ds(0, 7)], s2.at[1])
    for c in order:
        take(stages[c].at[pl.ds(0, pieces(c))], q_send.at[c])
    take(stage_low.at[pl.ds(0, 15)], l_send)
    for copy in sent + moves:
        copy.wait_send()
    for copy in to_pair:
        copy.wait_send()
    take(part.at[pl.ds(0, 63)], s2.at[2])
    take(part.at[pl.ds(0, 63)], r2.at[2])
    total = jnp.sum(part[...], axis=0)
    out_ref[...] = total * total


def per_device(
    eig_lower, eig_upper, layout_map, block_live, coupling, rot_coef, dip_zero, dip_raise, dip_lower
):
    smem = pl.BlockSpec(memory_space=pltpu.SMEM)
    vmem = pl.BlockSpec(memory_space=pltpu.VMEM)
    hbm = pl.BlockSpec(memory_space=pl.ANY)
    dma = pltpu.SemaphoreType.DMA
    out = pl.pallas_call(
        kernel,
        out_shape=jax.ShapeDtypeStruct((8, 128), F32),
        in_specs=[smem] * 3 + [hbm] * 6,
        out_specs=vmem,
        scratch_shapes=[
            pltpu.VMEM((512, 128), jnp.int32),
            pltpu.VMEM((1, 512), jnp.int32),
            pltpu.SMEM((1, 512), jnp.int32),
            pltpu.VMEM((64, 8, 512), BF16),
            pltpu.VMEM((32, 8, 512), BF16),
            pltpu.VMEM((128, 8, 128), BF16),
            pltpu.VMEM((128, 8, 128), BF16),
            pltpu.VMEM((16, 8, 2, 8, 128), BF16),
            pltpu.VMEM((16, 8, 2, 8, 128), BF16),
            pltpu.VMEM((16, 8, 2, 8, 128), BF16),
            *[pltpu.VMEM((8, 16, w), BF16) for w in WIDTHS],
            *[pltpu.VMEM((4, 2, 4, 4, 16, w), BF16) for w in WIDTHS],
            pltpu.VMEM((16, 2, 16, 512), BF16),
            pltpu.VMEM((16, 2, 16, 512), BF16),
            pltpu.VMEM((2, 2, 2, 16, 16, 512), BF16),
            pltpu.VMEM((3, 256, 2048), BF16),
            pltpu.VMEM((3, 4, 2, 4, 64, 256), F32),
            pltpu.VMEM((256, 2048), BF16),
            pltpu.VMEM((2, 2, 32, 8, 128), F32),
            pltpu.VMEM((2, 32, 8, 128), F32),
            pltpu.VMEM((64, 8, 128), F32),
            pltpu.SemaphoreType.REGULAR,
            dma((4,)), dma((3,)),
            dma((4,)), dma((4,)), dma((3,)), dma((3,)),
            dma((CHAINS,)), dma((CHAINS,)),
            dma((CHAINS, 12)), dma((CHAINS, 12)),
            dma, dma,
            dma((4,)), dma((4,)),
        ],
        compiler_params=pltpu.CompilerParams(
            collective_id=0, has_side_effects=True, vmem_limit_bytes=60 * 1024 * 1024
        ),
        cost_estimate=pl.CostEstimate(flops=7_000_000_000, bytes_accessed=5_000_000, transcendentals=0),
    )(
        block_live, coupling.T, rot_coef.T, layout_map.reshape(512, 128),
        eig_lower.reshape(64, 8, 512), eig_upper.reshape(32, 8, 512), dip_zero, dip_raise, dip_lower,
    )
    return out.T


def solution(mesh):
    return jax.shard_map(
        per_device,
        mesh=mesh,
        in_specs=(
            P(None, ("ka", "vert")),
            P(None, ("ka", "vert")),
            P(),
            P(),
            P(),
            P(),
            P("vert", "ka"),
            P("vert", "ka"),
            P("vert", "ka"),
        ),
        out_specs=P("ka", "vert"),
        check_vma=False,
    )
```
